32 devices in a mesh: real: 8 (over y, x, core), site: 4 (over z).
Axes of the slice: x: 2, y: 2, z: 4, core: 2. Of those that a mesh axis runs over, the one named last changes fastest.
Arguments:
- noise: bfloat16 [4096, 6144], P('site', 'real'), may hold values from -6 to 6
- v_factors: bfloat16 [4, 1024, 1024], P('site', 'real'), may hold values from -0.1875 to 0.1875
- u_factors: bfloat16 [4, 1024, 1024], P('site', 'real'), may hold values from -0.1875 to 0.1875
- ranks: int32 [4, 4], replicated, may hold values from 1 to 2, as said below
- skew_g: float32 [4096], P('site'), may hold values from 0.1 to 0.6
- tail_h: float32 [4096], P('site'), may hold values from 0.05 to 0.3
Outputs:
- field: float32 [4096, 6144], P('site', 'real')
The draws below stay inside these ranges and needn't reach their ends.
Inputs may be any that keep to these rules, and one draw needn't show every extreme that they name: `ranks`: every tile has at least one rank block, and some tile has 2.
All inputs are finite; a program needn't handle non-finite values.
Results may differ from the reference program's by a relative error of at most 0.012.
The reference program's roundings to bfloat16 on the way (of `coef`) count: a program that leaves them out, or rounds other values in their place, can miss the bound.
Values may be sent and summed in bfloat16 or wider, within the bound.
No kernel may reach another device: no remote copies, remote signals or barrier semaphores. Data moves between devices by JAX's collectives and lax.ppermute only.
A program may use at most 128 MiB of HBM per device.

```python
import math
import jax
import jax.numpy as jnp
from jax import lax

TILE = 1024
RANKB = 128
CAP = 2
SITES = 4096
REALS = 6144
RANK_COLS = 1024
N_SITE = 4


def draw_ranks(key, part):
    first_key, second_key = jax.random.split(jax.random.fold_in(key, 11))
    base = jax.random.randint(first_key, (N_SITE * N_SITE,), 1, CAP + 1)
    chosen = jax.random.randint(second_key, (), 0, N_SITE * N_SITE)
    filled = jnp.where(jnp.arange(N_SITE * N_SITE) == chosen, CAP, base)
    return filled.reshape(N_SITE, N_SITE).astype(jnp.int32)


def steps_of(rng, shape, pieces, least, top_value):
    loudness, own = 1.0, jax.random.fold_in(rng, 6)
    for axis_at, shards_of in pieces:
        draws = jnp.exp(jax.random.uniform(jax.random.fold_in(own, axis_at), (shards_of,), jnp.float32, least / len(pieces), top_value / len(pieces)))
        loudness = loudness * jnp.repeat(draws, shape[axis_at] // shards_of).reshape([-1 if axis == axis_at else 1 for axis in range(len(shape))])
    return loudness


def bell_draw(key, dims, spread, limit, shards=(), kind=jnp.bfloat16):
    values = jax.random.normal(key, dims, jnp.float32) * spread
    if len(shards) > 0:
        values = steps_of(key, dims, shards, -0.22, 0.18) * values
    return jnp.clip(values, min=-limit, max=limit).astype(kind)


def setup_inputs(seed: int = 0) -> dict:
    key_of = jax.random.split(jax.random.key(seed), 7)
    return {
        "noise": bell_draw(key_of[0], (SITES, REALS), 1.0, 6.0, ((0, 4), (1, 8))),
        "v_factors": bell_draw(key_of[1], (N_SITE, TILE, RANK_COLS), TILE ** -0.5, 0.1875, ((0, 4), (1, 8))),
        "u_factors": bell_draw(key_of[2], (N_SITE, TILE, RANK_COLS), RANK_COLS ** -0.5, 0.1875, ((0, 4), (1, 8))),
        "ranks": draw_ranks(jax.random.fold_in(key_of[6], 71), 0),
        "skew_g": jnp.clip(jnp.exp(math.log(0.6) - 1.7917595 * jax.random.uniform(key_of[4], (SITES,), jnp.float32) ** steps_of(key_of[4], (SITES,), ((0, 4),), -0.2, 0.2)), 0.1, 0.6),
        "tail_h": jnp.clip(0.05 + 0.25 * jax.random.uniform(key_of[5], (SITES,), jnp.float32) ** steps_of(key_of[5], (SITES,), ((0, 4),), -0.2, 0.2), 0.05, 0.3),
    }


def reference(noise, v_factors, u_factors, ranks, skew_g, tail_h):
    per_tile = CAP * RANKB
    levels = jnp.arange(CAP, dtype=jnp.int32)
    alive = (levels[None, None, :] < jnp.transpose(ranks)[:, :, None]).astype(jnp.float32)
    noise_tiles = noise.reshape(N_SITE, TILE, -1)
    u_by_source = jnp.transpose(u_factors.reshape(N_SITE, TILE, N_SITE, per_tile), (2, 0, 1, 3))

    def add_source(running, inputs):
        v_tile, noise_tile, alive_col, u_tiles = inputs
        projected = lax.dot_general(v_tile, noise_tile, (((0,), (0,)), ((), ())), preferred_element_type=jnp.float32)
        masked = projected.reshape(N_SITE, CAP, RANKB, -1) * alive_col[:, :, None, None]
        coef = masked.astype(jnp.bfloat16).reshape(N_SITE, per_tile, -1)
        contrib = jnp.einsum("itr,irn->itn", u_tiles.astype(jnp.float32), coef.astype(jnp.float32),
                             precision=lax.Precision.HIGHEST)
        return running + contrib.reshape(N_SITE * TILE, -1), None

    start_sum = jnp.zeros((N_SITE * TILE, noise.shape[1]), jnp.float32)
    gaussian, _ = lax.scan(add_source, start_sum, (v_factors, noise_tiles, alive, u_by_source))
    skew_col = skew_g[:, None]
    tail_col = tail_h[:, None]
    return jnp.expm1(skew_col * gaussian) / skew_col * jnp.exp(0.5 * tail_col * gaussian * gaussian)
```

```python
import functools

import jax
import jax.numpy as jnp
from jax import lax
from jax.experimental import pallas as pl
from jax.experimental.pallas import tpu as pltpu
from jax.sharding import PartitionSpec as P

CAP = 2


def project_kernel(shifts, n_pieces, ranks_ref, noise_ref, *refs):
    pieces, outs, whole = refs[:n_pieces], refs[n_pieces:-1], refs[-1]
    site_count = lax.axis_size("site")
    source = lax.axis_index("site")
    me = lax.axis_index("real")
    rows = pieces[0].shape[0]
    for distance, piece in enumerate(pieces):
        start = pl.multiple_of((me ^ distance) * rows, rows)
        whole[pl.ds(start, rows), :] = piece[...]
    for place, (shift, out_ref) in enumerate(zip(shifts, outs)):
        target = lax.rem(source + shift, site_count)
        columns = out_ref.shape[0]
        projected = lax.dot_general(
            whole[:, place * columns : (place + 1) * columns],
            noise_ref[...],
            (((0,), (0,)), ((), ())),
            preferred_element_type=jnp.float32,
        )
        rank = ranks_ref[target, source]
        block = columns // CAP
        for level in range(CAP):
            part = projected[level * block : (level + 1) * block]
            part = part * jnp.where(level < rank, 1.0, 0.0)
            out_ref[level * block : (level + 1) * block, :] = part.astype(out_ref.dtype)


def project(shifts, ranks, noise, pieces):
    sites, reals = noise.shape
    columns = pieces[0].shape[1]
    return pl.pallas_call(
        functools.partial(project_kernel, shifts, len(pieces)),
        out_shape=[jax.ShapeDtypeStruct((columns // len(shifts), reals), jnp.bfloat16)]
        * len(shifts),
        in_specs=[pl.BlockSpec(memory_space=pltpu.SMEM)]
        + [pl.BlockSpec(memory_space=pltpu.VMEM)] * (1 + len(pieces)),
        out_specs=[pl.BlockSpec(memory_space=pltpu.VMEM)] * len(shifts),
        scratch_shapes=[pltpu.VMEM((sites, columns), jnp.bfloat16)],
        compiler_params=pltpu.CompilerParams(vmem_limit_bytes=44 * 2**20),
        cost_estimate=pl.CostEstimate(
            flops=2 * sites * columns * reals,
            bytes_accessed=2 * (sites * columns + sites * reals + columns * reals),
            transcendentals=0,
        ),
        name=f"project_{len(shifts)}",
    )(ranks, noise, *pieces)


def finish_kernel(shifts, u_ref, skew_ref, tail_ref, *refs):
    coefs, out_ref = refs[: len(shifts)], refs[len(shifts)]
    site_count = lax.axis_size("site")
    target = lax.axis_index("site")
    gaussian = jnp.zeros(out_ref.shape, jnp.float32)
    for shift, coef in zip(shifts, coefs):
        columns = coef.shape[0]
        source = lax.rem(target + (site_count - shift), site_count)
        start = pl.multiple_of(source * columns, columns)
        gaussian += jnp.dot(
            u_ref[:, pl.ds(start, columns)], coef[...], preferred_element_type=jnp.float32
        )
    skew, tail = skew_ref[...], tail_ref[...]
    scaled = skew * gaussian
    series = 1.0 + scaled * (0.5 + scaled * (1 / 6 + scaled * (1 / 24 + scaled * (1 / 120))))
    grown = jnp.where(jnp.abs(scaled) < 0.125, scaled * series, jnp.exp(scaled) - 1.0)
    out_ref[...] = grown * (1.0 / skew) * jnp.exp((0.5 * tail) * gaussian * gaussian)


def finish(shifts, u_whole, skew, tail, coefs):
    rows, columns = u_whole.shape
    reals = coefs[0].shape[1]
    block = min(rows, 256)
    by_row = lambda i: (i, 0)
    fixed = lambda i: (0, 0)
    return pl.pallas_call(
        functools.partial(finish_kernel, shifts),
        out_shape=jax.ShapeDtypeStruct((rows, reals), jnp.float32),
        grid=(rows // block,),
        in_specs=[
            pl.BlockSpec((block, columns), by_row),
            pl.BlockSpec((block, 1), by_row),
            pl.BlockSpec((block, 1), by_row),
        ]
        + [pl.BlockSpec(coef.shape, fixed) for coef in coefs],
        out_specs=pl.BlockSpec((block, reals), by_row),
        compiler_params=pltpu.CompilerParams(vmem_limit_bytes=40 * 2**20),
        cost_estimate=pl.CostEstimate(
            flops=2 * rows * columns * reals,
            bytes_accessed=2 * rows * columns + 2 * columns * reals + 4 * rows * reals,
            transcendentals=2 * rows * reals,
        ),
        name="finish",
    )(u_whole, skew, tail, *coefs)


def gather_pieces(own, count):
    pieces = {0: own}
    for distance in range(2, count, 2):
        pieces[distance] = lax.ppermute(own, "real", [(k, k ^ distance) for k in range(count)])
    for distance in range(0, count, 2):
        pieces[distance + 1] = lax.ppermute(
            pieces[distance], "real", [(k, k ^ 1) for k in range(count)]
        )
    return [pieces[distance] for distance in range(count)]


def per_device(noise, v_factors, u_factors, ranks, skew_g, tail_h):
    site_count = lax.axis_size("site")
    real_count = lax.axis_size("real")
    source = lax.axis_index("site")
    rows, columns = v_factors.shape[1:]
    per_dest = columns // site_count
    middle = site_count // 2
    shifts = [middle]
    for step in range(1, site_count):
        for shift in (middle - step, middle + step):
            if 0 < shift < site_count and shift not in shifts:
                shifts.append(shift)
    shifts.append(0)
    coefs = []
    done = v_factors
    for group in (shifts[:1], shifts[1:]):
        v_own = lax.optimization_barrier((v_factors, done))[0][0]
        own = jnp.concatenate(
            [
                lax.dynamic_slice(
                    v_own, (0, lax.rem(source + shift, site_count) * per_dest), (rows, per_dest)
                )
                for shift in group
            ],
            axis=1,
        )
        group_coefs = project(tuple(group), ranks, noise, gather_pieces(own, real_count))
        done = group_coefs[0]
        for shift, coef in zip(group, group_coefs):
            if shift:
                coef = lax.ppermute(
                    coef, "site", [(k, (k + shift) % site_count) for k in range(site_count)]
                )
            coefs.append(coef)
    u_whole = lax.all_gather(u_factors, "real", axis=1, tiled=True)[0]
    return finish(tuple(shifts), u_whole, skew_g[:, None], tail_h[:, None], coefs)


def solution(mesh):
    placed = (
        P("site", "real"),
        P("site", "real", None),
        P("site", "real", None),
        P(),
        P("site"),
        P("site"),
    )
    return jax.shard_map(
        per_device, mesh=mesh, in_specs=placed, out_specs=P("site", "real"), check_vma=False
    )
```

```python
import functools

import jax
import jax.numpy as jnp
from jax import lax
from jax.experimental import pallas as pl
from jax.experimental.pallas import tpu as pltpu
from jax.sharding import PartitionSpec as P

CAP = 2
VMEM = pl.BlockSpec(memory_space=pltpu.VMEM)
SMEM = pl.BlockSpec(memory_space=pltpu.SMEM)
LIMIT = pltpu.CompilerParams(vmem_limit_bytes=44 * 2**20)


def stack_pieces(pieces, whole):
    me = lax.axis_index("real")
    rows = pieces[0].shape[0]
    for distance, piece in enumerate(pieces):
        start = pl.multiple_of((me ^ distance) * rows, rows)
        whole[pl.ds(start, rows), :] = piece[...]


def project_kernel(n_pieces, noise_ref, *refs):
    pieces, outs, whole = refs[:n_pieces], refs[n_pieces:-1], refs[-1]
    stack_pieces(pieces, whole)
    for place, out_ref in enumerate(outs):
        columns = out_ref.shape[0]
        projected = lax.dot_general(
            whole[:, place * columns : (place + 1) * columns],
            noise_ref[...],
            (((0,), (0,)), ((), ())),
            preferred_element_type=jnp.float32,
        )
        out_ref[...] = projected.astype(out_ref.dtype)


def project(n_shifts, noise, pieces):
    sites, reals = noise.shape
    columns = pieces[0].shape[1]
    return pl.pallas_call(
        functools.partial(project_kernel, len(pieces)),
        out_shape=[jax.ShapeDtypeStruct((columns // n_shifts, reals), jnp.bfloat16)] * n_shifts,
        in_specs=[VMEM] * (1 + len(pieces)),
        out_specs=[VMEM] * n_shifts,
        scratch_shapes=[pltpu.VMEM((sites, columns), jnp.bfloat16)],
        compiler_params=LIMIT,
        cost_estimate=pl.CostEstimate(
            flops=2 * sites * columns * reals,
            bytes_accessed=2 * (sites * columns + sites * reals + columns * reals),
            transcendentals=0,
        ),
        name=f"project_{n_shifts}",
    )(noise, *pieces)


def stage_kernel(from_ref, to_ref, sems):
    parts = sems.shape[0]
    rows = from_ref.shape[0] // parts
    copies = []
    for part in range(parts):
        span = slice(part * rows, (part + 1) * rows)
        copies.append(
            pltpu.make_async_copy(from_ref.at[span, :], to_ref.at[span, :], sems.at[part])
        )
        copies[-1].start()
    for copy in copies:
        copy.wait()


def stage(array):
    return pl.pallas_call(
        stage_kernel,
        out_shape=jax.ShapeDtypeStruct(array.shape, array.dtype),
        in_specs=[pl.BlockSpec(memory_space=pltpu.HBM)],
        out_specs=VMEM,
        scratch_shapes=[pltpu.SemaphoreType.DMA((4,))],
        compiler_params=LIMIT,
        cost_estimate=pl.CostEstimate(
            flops=0, bytes_accessed=2 * array.size * array.dtype.itemsize, transcendentals=0
        ),
        name="stage",
    )(array)


def source_of(shift):
    site_count = lax.axis_size("site")
    return lax.rem(lax.axis_index("site") + (site_count - shift), site_count)


def alive_coef(shift, ranks_ref, coef_ref):
    rank = ranks_ref[lax.axis_index("site"), source_of(shift)]
    block = coef_ref.shape[0] // CAP
    row = lax.broadcasted_iota(jnp.int32, coef_ref.shape, 0)
    return jnp.where(row < rank * block, coef_ref[...].astype(jnp.float32), 0.0).astype(
        coef_ref.dtype
    )


def accumulate_kernel(shifts, ranks_ref, u_ref, *refs):
    coefs, sum_ref = refs[: len(shifts)], refs[-1]
    total = None
    for shift, coef_ref in zip(shifts, coefs):
        columns = coef_ref.shape[0]
        start = pl.multiple_of(source_of(shift) * columns, columns)
        term = jnp.dot(
            u_ref[:, pl.ds(start, columns)],
            alive_coef(shift, ranks_ref, coef_ref),
            preferred_element_type=jnp.float32,
        )
        total = term if total is None else total + term
    sum_ref[...] = total


def accumulate(shifts, ranks, u_whole, coefs):
    sites, columns = u_whole.shape
    per_source, reals = coefs[0].shape
    return pl.pallas_call(
        functools.partial(accumulate_kernel, shifts),
        out_shape=jax.ShapeDtypeStruct((sites, reals), jnp.float32),
        in_specs=[SMEM] + [VMEM] * (1 + len(coefs)),
        out_specs=VMEM,
        compiler_params=LIMIT,
        cost_estimate=pl.CostEstimate(
            flops=2 * sites * per_source * len(shifts) * reals,
            bytes_accessed=2 * sites * columns + 4 * sites * reals,
            transcendentals=0,
        ),
        name="accumulate",
    )(ranks, u_whole, *coefs)


def finish_kernel(shifts, ranks_ref, u_ref, sum_ref, skew_ref, tail_ref, *refs):
    coefs = refs[: len(shifts)]
    out_ref, slots, sems = refs[len(shifts) :]
    block = slots.shape[1]
    alive = [alive_coef(shift, ranks_ref, coef) for shift, coef in zip(shifts, coefs)]
    copies = []
    for step in range(out_ref.shape[0] // block):
        rows = slice(step * block, (step + 1) * block)
        gaussian = sum_ref[rows, :]
        for shift, coef in zip(shifts, alive):
            columns = coef.shape[0]
            start = pl.multiple_of(source_of(shift) * columns, columns)
            gaussian += jnp.dot(
                u_ref[rows, pl.ds(start, columns)], coef, preferred_element_type=jnp.float32
            )
        skew, tail = skew_ref[rows, :], tail_ref[rows, :]
        scaled = skew * gaussian
        series = 1.0 + scaled * (0.5 + scaled * (1 / 6 + scaled * (1 / 24 + scaled * (1 / 120))))
        grown = jnp.where(jnp.abs(scaled) < 0.125, scaled * series, jnp.exp(scaled) - 1.0)
        slots[step] = grown * (1.0 / skew) * jnp.exp((0.5 * tail) * gaussian * gaussian)
        copy = pltpu.make_async_copy(slots.at[step], out_ref.at[rows, :], sems.at[step])
        copy.start()
        copies.append(copy)
    for copy in copies:
        copy.wait()


def finish(shifts, ranks, u_whole, total, skew, tail, coefs):
    rows, columns = u_whole.shape
    per_source, reals = coefs[0].shape
    block = min(rows, 128)
    return pl.pallas_call(
        functools.partial(finish_kernel, shifts),
        out_shape=jax.ShapeDtypeStruct((rows, reals), jnp.float32),
        in_specs=[SMEM] + [VMEM] * (4 + len(coefs)),
        out_specs=pl.BlockSpec(memory_space=pl.ANY),
        scratch_shapes=[
            pltpu.VMEM((rows // block, block, reals), jnp.float32),
            pltpu.SemaphoreType.DMA((rows // block,)),
        ],
        compiler_params=LIMIT,
        cost_estimate=pl.CostEstimate(
            flops=2 * rows * per_source * len(shifts) * reals,
            bytes_accessed=2 * rows * columns + 8 * rows * reals,
            transcendentals=2 * rows * reals,
        ),
        name="finish",
    )(ranks, u_whole, total, skew, tail, *coefs)


def after(value, *before):
    return lax.optimization_barrier((value, before))[0]


def from_chips(own, count):
    pieces = {0: own}
    for distance in range(2, count, 2):
        pieces[distance] = lax.ppermute(own, "real", [(k, k ^ distance) for k in range(count)])
    return pieces


def from_core(pieces, count):
    swapped = {
        distance ^ 1: lax.ppermute(piece, "real", [(k, k ^ 1) for k in range(count)])
        for distance, piece in pieces.items()
    }
    return [{**pieces, **swapped}[distance] for distance in range(count)]


def along_site(coef, shift):
    count = lax.axis_size("site")
    return lax.ppermute(coef, "site", [(k, (k + shift) % count) for k in range(count)])


def per_device(noise, v_factors, u_factors, ranks, skew_g, tail_h):
    site_count = lax.axis_size("site")
    real_count = lax.axis_size("real")
    source = lax.axis_index("site")
    rows, columns = v_factors.shape[1:]
    per_dest = columns // site_count
    middle = site_count // 2
    others = sorted(range(1, site_count), key=lambda shift: (abs(shift - middle), shift))
    first, rest = others[:1], others[1:] + [0]

    def columns_for(shift):
        start = lax.rem(source + shift, site_count) * per_dest
        return lax.dynamic_slice(v_factors[0], (0, start), (rows, per_dest))

    v_first = from_chips(columns_for(first[0]), real_count)
    v_rest = jnp.concatenate([columns_for(shift) for shift in rest], axis=1)
    noise = stage(noise)
    v_first = after(v_first, noise, v_rest)
    arrived = list(v_first.values())[1:]
    u_mine = after(u_factors, *arrived)
    u_whole = lax.all_gather(u_mine, "real", axis=1, tiled=True)[0]
    v_rest = from_chips(after(v_rest, *arrived), real_count)
    coefs = dict(zip(first, project(len(first), noise, from_core(v_first, real_count))))
    v_rest = after(v_rest, coefs[first[0]])
    coefs.update(zip(rest, project(len(rest), noise, from_core(v_rest, real_count))))
    received = {shift: along_site(coef, shift) if shift else coef for shift, coef in coefs.items()}
    early, late = (0, first[0]), tuple(rest[:-1])
    total = accumulate(early, ranks, u_whole, [received[shift] for shift in early])
    return finish(
        late, ranks, u_whole, total, skew_g[:, None], tail_h[:, None], [received[s] for s in late]
    )


def solution(mesh):
    placed = (
        P("site", "real"),
        P("site", "real", None),
        P("site", "real", None),
        P(),
        P("site"),
        P("site"),
    )
    return jax.shard_map(
        per_device, mesh=mesh, in_specs=placed, out_specs=P("site", "real"), check_vma=False
    )
```

```python
import functools

import jax
import jax.numpy as jnp
from jax import lax
from jax.experimental import pallas as pl
from jax.experimental.pallas import tpu as pltpu
from jax.sharding import PartitionSpec as P

CAP = 2
VMEM = pl.BlockSpec(memory_space=pltpu.VMEM)
SMEM = pl.BlockSpec(memory_space=pltpu.SMEM)
LIMIT = pltpu.CompilerParams(vmem_limit_bytes=44 * 2**20)


def stack_pieces(pieces, whole):
    me = lax.axis_index("real")
    rows = pieces[0].shape[0]
    for distance, piece in enumerate(pieces):
        start = pl.multiple_of((me ^ distance) * rows, rows)
        whole[pl.ds(start, rows), :] = piece[...]


def project_kernel(n_pieces, noise_ref, *refs):
    pieces, outs, whole = refs[:n_pieces], refs[n_pieces:-1], refs[-1]
    stack_pieces(pieces, whole)
    for place, out_ref in enumerate(outs):
        columns = out_ref.shape[0]
        projected = lax.dot_general(
            whole[:, place * columns : (place + 1) * columns],
            noise_ref[...],
            (((0,), (0,)), ((), ())),
            preferred_element_type=jnp.float32,
        )
        out_ref[...] = projected.astype(out_ref.dtype)


def project(n_shifts, noise, pieces):
    sites, reals = noise.shape
    columns = pieces[0].shape[1]
    return pl.pallas_call(
        functools.partial(project_kernel, len(pieces)),
        out_shape=[jax.ShapeDtypeStruct((columns // n_shifts, reals), jnp.bfloat16)] * n_shifts,
        in_specs=[VMEM] * (1 + len(pieces)),
        out_specs=[VMEM] * n_shifts,
        scratch_shapes=[pltpu.VMEM((sites, columns), jnp.bfloat16)],
        compiler_params=LIMIT,
        cost_estimate=pl.CostEstimate(
            flops=2 * sites * columns * reals,
            bytes_accessed=2 * (sites * columns + sites * reals + columns * reals),
            transcendentals=0,
        ),
        name=f"project_{n_shifts}",
    )(noise, *pieces)


def stage_kernel(from_ref, to_ref, sems):
    parts = sems.shape[0]
    rows = from_ref.shape[0] // parts
    copies = []
    for part in range(parts):
        span = slice(part * rows, (part + 1) * rows)
        copies.append(
            pltpu.make_async_copy(from_ref.at[span, :], to_ref.at[span, :], sems.at[part])
        )
        copies[-1].start()
    for copy in copies:
        copy.wait()


def stage(array):
    return pl.pallas_call(
        stage_kernel,
        out_shape=jax.ShapeDtypeStruct(array.shape, array.dtype),
        in_specs=[pl.BlockSpec(memory_space=pltpu.HBM)],
        out_specs=VMEM,
        scratch_shapes=[pltpu.SemaphoreType.DMA((4,))],
        compiler_params=LIMIT,
        cost_estimate=pl.CostEstimate(
            flops=0, bytes_accessed=2 * array.size * array.dtype.itemsize, transcendentals=0
        ),
        name="stage",
    )(array)


def source_of(shift):
    site_count = lax.axis_size("site")
    return lax.rem(lax.axis_index("site") + (site_count - shift), site_count)


def alive_coef(shift, ranks_ref, coef_ref):
    rank = ranks_ref[lax.axis_index("site"), source_of(shift)]
    block = coef_ref.shape[0] // CAP
    row = lax.broadcasted_iota(jnp.int32, coef_ref.shape, 0)
    return jnp.where(row < rank * block, coef_ref[...].astype(jnp.float32), 0.0).astype(
        coef_ref.dtype
    )


def accumulate_kernel(shifts, n_pieces, ranks_ref, *refs):
    pieces, coefs = refs[:n_pieces], refs[n_pieces : n_pieces + len(shifts)]
    whole, sum_ref = refs[-2:]
    stack_pieces(pieces, whole)
    total = None
    for shift, coef_ref in zip(shifts, coefs):
        columns = coef_ref.shape[0]
        start = pl.multiple_of(source_of(shift) * columns, columns)
        term = jnp.dot(
            whole[:, pl.ds(start, columns)],
            alive_coef(shift, ranks_ref, coef_ref),
            preferred_element_type=jnp.float32,
        )
        total = term if total is None else total + term
    sum_ref[...] = total


def accumulate(shifts, ranks, pieces, coefs):
    rows, columns = pieces[0].shape
    sites = rows * len(pieces)
    per_source, reals = coefs[0].shape
    return pl.pallas_call(
        functools.partial(accumulate_kernel, shifts, len(pieces)),
        out_shape=[
            jax.ShapeDtypeStruct((sites, columns), jnp.bfloat16),
            jax.ShapeDtypeStruct((sites, reals), jnp.float32),
        ],
        in_specs=[SMEM] + [VMEM] * (len(pieces) + len(coefs)),
        out_specs=[VMEM] * 2,
        compiler_params=LIMIT,
        cost_estimate=pl.CostEstimate(
            flops=2 * sites * per_source * len(shifts) * reals,
            bytes_accessed=4 * sites * columns + 4 * sites * reals,
            transcendentals=0,
        ),
        name="accumulate",
    )(ranks, *pieces, *coefs)


def finish_kernel(shifts, ranks_ref, u_ref, sum_ref, skew_ref, tail_ref, *refs):
    coefs = refs[: len(shifts)]
    out_ref, slots, sems = refs[len(shifts) :]
    block = slots.shape[1]
    alive = [alive_coef(shift, ranks_ref, coef) for shift, coef in zip(shifts, coefs)]
    copies = []
    for step in range(out_ref.shape[0] // block):
        rows = slice(step * block, (step + 1) * block)
        gaussian = sum_ref[rows, :]
        for shift, coef in zip(shifts, alive):
            columns = coef.shape[0]
            start = pl.multiple_of(source_of(shift) * columns, columns)
            gaussian += jnp.dot(
                u_ref[rows, pl.ds(start, columns)], coef, preferred_element_type=jnp.float32
            )
        skew, tail = skew_ref[rows, :], tail_ref[rows, :]
        scaled = skew * gaussian
        series = 1.0 + scaled * (0.5 + scaled * (1 / 6 + scaled * (1 / 24 + scaled * (1 / 120))))
        grown = jnp.where(jnp.abs(scaled) < 0.125, scaled * series, jnp.exp(scaled) - 1.0)
        slots[step] = grown * (1.0 / skew) * jnp.exp((0.5 * tail) * gaussian * gaussian)
        copy = pltpu.make_async_copy(slots.at[step], out_ref.at[rows, :], sems.at[step])
        copy.start()
        copies.append(copy)
    for copy in copies:
        copy.wait()


def finish(shifts, ranks, u_whole, total, skew, tail, coefs):
    rows, columns = u_whole.shape
    per_source, reals = coefs[0].shape
    block = min(rows, 128)
    return pl.pallas_call(
        functools.partial(finish_kernel, shifts),
        out_shape=jax.ShapeDtypeStruct((rows, reals), jnp.float32),
        in_specs=[SMEM] + [VMEM] * (4 + len(coefs)),
        out_specs=pl.BlockSpec(memory_space=pl.ANY),
        scratch_shapes=[
            pltpu.VMEM((rows // block, block, reals), jnp.float32),
            pltpu.SemaphoreType.DMA((rows // block,)),
        ],
        compiler_params=LIMIT,
        cost_estimate=pl.CostEstimate(
            flops=2 * rows * per_source * len(shifts) * reals,
            bytes_accessed=2 * rows * columns + 8 * rows * reals,
            transcendentals=2 * rows * reals,
        ),
        name="finish",
    )(ranks, u_whole, total, skew, tail, *coefs)


def after(value, *before):
    return lax.optimization_barrier((value, before))[0]


def from_chips(own, count):
    pieces = {0: own}
    for distance in range(2, count, 2):
        pieces[distance] = lax.ppermute(own, "real", [(k, k ^ distance) for k in range(count)])
    return pieces


def from_core(pieces, count):
    swapped = {
        distance ^ 1: lax.ppermute(piece, "real", [(k, k ^ 1) for k in range(count)])
        for distance, piece in pieces.items()
    }
    return [{**pieces, **swapped}[distance] for distance in range(count)]


def gather_at_once(present, own, count):
    return [own] + lax.cond(
        present,
        lambda mine: from_core(from_chips(mine, count), count)[1:],
        lambda mine: [mine] * (count - 1),
        own,
    )


def along_site(coef, shift):
    count = lax.axis_size("site")
    return lax.ppermute(coef, "site", [(k, (k + shift) % count) for k in range(count)])


def per_device(noise, v_factors, u_factors, ranks, skew_g, tail_h):
    site_count = lax.axis_size("site")
    real_count = lax.axis_size("real")
    source = lax.axis_index("site")
    rows, columns = v_factors.shape[1:]
    per_dest = columns // site_count
    middle = site_count // 2
    others = sorted(range(1, site_count), key=lambda shift: (abs(shift - middle), shift))
    first, rest = others[:1], others[1:] + [0]

    def columns_for(shift):
        start = lax.rem(source + shift, site_count) * per_dest
        return lax.dynamic_slice(v_factors[0], (0, start), (rows, per_dest))

    v_first = from_chips(columns_for(first[0]), real_count)
    v_rest = jnp.concatenate([columns_for(shift) for shift in rest], axis=1)
    noise = stage(noise)
    last = max(v_first)
    v_first[last], noise, v_rest = lax.optimization_barrier((v_first[last], noise, v_rest))
    coefs = dict(zip(first, project(len(first), noise, from_core(v_first, real_count))))

    present = ranks[0, 0] > 0
    v_rest = gather_at_once(present, after(v_rest, coefs[first[0]]), real_count)
    coefs.update(zip(rest, project(len(rest), noise, v_rest)))
    received = {shift: along_site(coef, shift) if shift else coef for shift, coef in coefs.items()}
    u_pieces = gather_at_once(present, after(u_factors[0], coefs[rest[0]]), real_count)

    early, late = (0, first[0]), tuple(rest[:-1])
    u_whole, total = accumulate(early, ranks, u_pieces, [received[shift] for shift in early])
    return finish(
        late, ranks, u_whole, total, skew_g[:, None], tail_h[:, None], [received[s] for s in late]
    )


def solution(mesh):
    placed = (
        P("site", "real"),
        P("site", "real", None),
        P("site", "real", None),
        P(),
        P("site"),
        P("site"),
    )
    return jax.shard_map(
        per_device, mesh=mesh, in_specs=placed, out_specs=P("site", "real"), check_vma=False
    )
```

```python
import functools

import jax
import jax.numpy as jnp
from jax import lax
from jax.experimental import pallas as pl
from jax.experimental.pallas import tpu as pltpu
from jax.sharding import PartitionSpec as P

CAP = 2
LOG2E = 1.4426950408889634
VMEM = pl.BlockSpec(memory_space=pltpu.VMEM)
SMEM = pl.BlockSpec(memory_space=pltpu.SMEM)
SMALL = pl.CostEstimate(flops=1, bytes_accessed=1, transcendentals=0)
LIMIT = pltpu.CompilerParams(vmem_limit_bytes=44 * 2**20)


def stack_pieces(places, rows, pieces, whole):
    me = lax.axis_index("real")
    for (distance, row), piece in zip(places, pieces):
        height = piece.shape[0]
        start = pl.multiple_of((me ^ distance) * rows + row, height)
        whole[pl.ds(start, height), :] = piece[...]


def project_columns(v_columns, noise_ref):
    projected = lax.dot_general(
        v_columns, noise_ref[...], (((0,), (0,)), ((), ())), preferred_element_type=jnp.float32
    )
    return projected.astype(jnp.bfloat16)


def project_kernel(places, rows, noise_ref, *refs):
    pieces, outs, whole = refs[: len(places)], refs[len(places) : -1], refs[-1]
    stack_pieces(places, rows, pieces, whole)
    for place, out_ref in enumerate(outs):
        columns = out_ref.shape[0]
        out_ref[...] = project_columns(
            whole[:, place * columns : (place + 1) * columns], noise_ref
        )


def project(n_shifts, noise, gathered):
    sites, reals = noise.shape
    places, pieces = zip(*gathered)
    rows, columns = pieces[0].shape
    return pl.pallas_call(
        functools.partial(project_kernel, places, rows),
        out_shape=[jax.ShapeDtypeStruct((columns // n_shifts, reals), jnp.bfloat16)] * n_shifts,
        in_specs=[VMEM] * (1 + len(pieces)),
        out_specs=[VMEM] * n_shifts,
        scratch_shapes=[pltpu.VMEM((sites, columns), jnp.bfloat16)],
        compiler_params=LIMIT,
        cost_estimate=SMALL,
        name=f"project_{n_shifts}",
    )(noise, *pieces)


def stage_kernel(from_ref, to_ref, sems):
    parts = sems.shape[0]
    rows = from_ref.shape[0] // parts
    copies = []
    for part in range(parts):
        span = slice(part * rows, (part + 1) * rows)
        copies.append(
            pltpu.make_async_copy(from_ref.at[span, :], to_ref.at[span, :], sems.at[part])
        )
        copies[-1].start()
    for copy in copies:
        copy.wait()


def stage(array):
    return pl.pallas_call(
        stage_kernel,
        out_shape=jax.ShapeDtypeStruct(array.shape, array.dtype),
        in_specs=[pl.BlockSpec(memory_space=pltpu.HBM)],
        out_specs=VMEM,
        scratch_shapes=[pltpu.SemaphoreType.DMA((4,))],
        compiler_params=LIMIT,
        cost_estimate=SMALL,
        name="stage",
    )(array)


def source_of(shift):
    site_count = lax.axis_size("site")
    return lax.rem(lax.axis_index("site") + (site_count - shift), site_count)


def alive_coef(shift, ranks_ref, coef):
    rank = ranks_ref[lax.axis_index("site"), source_of(shift)]
    row = lax.broadcasted_iota(jnp.int32, coef.shape, 0)
    alive = row < rank * (coef.shape[0] // CAP)
    return jnp.where(alive, coef.astype(jnp.float32), 0.0).astype(coef.dtype)


def accumulate_kernel(shifts, places, rows, ranks_ref, noise_ref, *refs):
    pieces, coefs = refs[: len(places)], refs[len(places) : len(places) + len(shifts)]
    u_ref, sum_ref, whole = refs[-3:]
    stack_pieces(places, rows, pieces, whole)
    per_source = whole.shape[1] - u_ref.shape[1]
    u_ref[...] = whole[:, per_source:]
    own = project_columns(whole[:, :per_source], noise_ref)
    total = jnp.zeros(sum_ref.shape, jnp.float32)
    for shift, coef in zip((0,) + shifts, [own] + [coef_ref[...] for coef_ref in coefs]):
        start = pl.multiple_of(source_of(shift) * per_source, per_source)
        total += jnp.dot(
            u_ref[:, pl.ds(start, per_source)],
            alive_coef(shift, ranks_ref, coef),
            preferred_element_type=jnp.float32,
        )
    sum_ref[...] = total


def accumulate(shifts, ranks, noise, gathered, coefs):
    places, pieces = zip(*gathered)
    rows, columns = pieces[0].shape
    sites, reals = noise.shape
    return pl.pallas_call(
        functools.partial(accumulate_kernel, shifts, places, rows),
        out_shape=[
            jax.ShapeDtypeStruct((sites, columns - coefs[0].shape[0]), jnp.bfloat16),
            jax.ShapeDtypeStruct((sites, reals), jnp.float32),
        ],
        in_specs=[SMEM] + [VMEM] * (1 + len(pieces) + len(coefs)),
        out_specs=[VMEM] * 2,
        scratch_shapes=[pltpu.VMEM((sites, columns), jnp.bfloat16)],
        compiler_params=LIMIT,
        cost_estimate=SMALL,
        name="accumulate",
    )(ranks, noise, *pieces, *coefs)


def finish_kernel(shifts, ranks_ref, u_ref, sum_ref, skew_ref, tail_ref, *refs):
    coefs = refs[: len(shifts)]
    out_ref, slots, sems = refs[len(shifts) :]
    block = slots.shape[1]
    alive = [alive_coef(shift, ranks_ref, coef[...]) for shift, coef in zip(shifts, coefs)]
    copies = []
    for step in range(out_ref.shape[0] // block):
        rows = slice(step * block, (step + 1) * block)
        gaussian = sum_ref[rows, :]
        for shift, coef in zip(shifts, alive):
            columns = coef.shape[0]
            start = pl.multiple_of(source_of(shift) * columns, columns)
            gaussian += jnp.dot(
                u_ref[rows, pl.ds(start, columns)], coef, preferred_element_type=jnp.float32
            )
        skew, tail = skew_ref[rows, :], tail_ref[rows, :]
        grown = jnp.exp2((skew * LOG2E) * gaussian) + 1.0
        grown = grown * jnp.tanh((0.5 * skew) * gaussian) * (1.0 / skew)
        slots[step] = grown * jnp.exp2((0.5 * LOG2E * tail) * (gaussian * gaussian))
        copy = pltpu.make_async_copy(slots.at[step], out_ref.at[rows, :], sems.at[step])
        copy.start()
        copies.append(copy)
    for copy in copies:
        copy.wait()


def finish(shifts, ranks, u_whole, total, skew, tail, coefs):
    rows, columns = u_whole.shape
    per_source, reals = coefs[0].shape
    block = min(rows, 128)
    return pl.pallas_call(
        functools.partial(finish_kernel, shifts),
        out_shape=jax.ShapeDtypeStruct((rows, reals), jnp.float32),
        in_specs=[SMEM] + [VMEM] * (4 + len(coefs)),
        out_specs=pl.BlockSpec(memory_space=pl.ANY),
        scratch_shapes=[
            pltpu.VMEM((rows // block, block, reals), jnp.float32),
            pltpu.SemaphoreType.DMA((rows // block,)),
        ],
        compiler_params=LIMIT,
        cost_estimate=SMALL,
        name="finish",
    )(ranks, u_whole, total, skew, tail, *coefs)


def after(value, *before):
    return lax.optimization_barrier((value, before))[0]


def swap(array, distance):
    count = lax.axis_size("real")
    return lax.ppermute(array, "real", [(k, k ^ distance) for k in range(count)])


def with_other_core(pieces):
    both = dict(pieces)
    for (distance, row), piece in pieces.items():
        if (distance ^ 1, row) not in pieces:
            both[distance ^ 1, row] = swap(piece, 1)
    return both


def from_chips(own):
    pieces = {(0, 0): own}
    for distance in range(2, lax.axis_size("real"), 2):
        pieces[distance, 0] = swap(own, distance)
    return pieces


def relay_steps(count):
    if count != 8:
        return (lambda pieces: from_chips(pieces[0, 0]), with_other_core)

    def neighbours(pieces):
        own = pieces[0, 0]
        return {(2, 0): swap(own, 2), (4, 0): swap(own, 4), (1, 0): swap(own, 1)}

    def opposite(pieces):
        first, second = pieces[2, 0], pieces[4, 0]
        half = first.shape[0] // 2
        return {
            (6, 0): swap(second[:half], 2),
            (6, half): swap(first[half:], 4),
            (3, 0): swap(first, 1),
        }

    return (neighbours, opposite, with_other_core)


def at_once(present, gather, *arrays):
    shapes = jax.eval_shape(gather, *arrays)
    return lax.cond(
        present, gather, lambda *same: [same[0][: shape.shape[0]] for shape in shapes], *arrays
    )


def gather_at_once(present, own, steps):
    pieces = {(0, 0): own}
    for step in steps:
        places, arrays = list(pieces), list(pieces.values())
        new = []

        def added(*arrays):
            more = step(dict(zip(places, arrays)))
            new[:] = [place for place in more if place not in pieces]
            return [more[place] for place in new]

        results = at_once(present, added, *arrays)
        pieces.update(zip(new, results))
    return list(pieces.items())


def along_site(coef, shift):
    count = lax.axis_size("site")
    return lax.ppermute(coef, "site", [(k, (k + shift) % count) for k in range(count)])


def per_device(noise, v_factors, u_factors, ranks, skew_g, tail_h):
    site_count = lax.axis_size("site")
    real_count = lax.axis_size("real")
    source = lax.axis_index("site")
    rows, columns = v_factors.shape[1:]
    per_dest = columns // site_count
    middle = site_count // 2
    others = sorted(range(1, site_count), key=lambda shift: (abs(shift - middle), shift))
    first, rest = others[0], tuple(others[1:])

    def columns_for(shift):
        start = lax.rem(source + shift, site_count) * per_dest
        return lax.dynamic_slice(v_factors[0], (0, start), (rows, per_dest))

    v_first = columns_for(first)
    v_rest = jnp.concatenate([columns_for(shift) for shift in rest], axis=1)
    own_and_u = jnp.concatenate([columns_for(0), u_factors[0]], axis=1)
    present = ranks[0, 0] > 0
    v_first = from_chips(v_first)
    last = max(v_first)
    waiting = (v_first[last], stage(noise), v_rest, own_and_u, present)
    v_first[last], noise, v_rest, own_and_u, present = lax.optimization_barrier(waiting)
    coefs = {}
    [coefs[first]] = project(1, noise, list(with_other_core(v_first).items()))

    v_rest = after(v_rest, coefs[first])
    direct = (lambda pieces: with_other_core(from_chips(pieces[0, 0])),)
    v_rest = gather_at_once(present, v_rest, direct)
    coefs.update(zip(rest, project(len(rest), noise, v_rest)))
    received = {shift: along_site(coef, shift) for shift, coef in coefs.items()}

    own_and_u = after(own_and_u, coefs[rest[0]], received[first])
    own_and_u = gather_at_once(present, own_and_u, relay_steps(lax.axis_size("real")))
    u_whole, total = accumulate((first,), ranks, noise, own_and_u, [received[first]])
    return finish(
        rest, ranks, u_whole, total, skew_g[:, None], tail_h[:, None], [received[s] for s in rest]
    )


def solution(mesh):
    placed = (
        P("site", "real"),
        P("site", "real", None),
        P("site", "real", None),
        P(),
        P("site"),
        P("site"),
    )
    return jax.shard_map(
        per_device, mesh=mesh, in_specs=placed, out_specs=P("site", "real"), check_vma=False
    )
```

```python
import functools

import jax
import jax.numpy as jnp
from jax import lax
from jax.experimental import pallas as pl
from jax.experimental.pallas import tpu as pltpu
from jax.sharding import PartitionSpec as P

CAP = 2
LOG2E = 1.4426950408889634
VMEM = pl.BlockSpec(memory_space=pltpu.VMEM)
SMEM = pl.BlockSpec(memory_space=pltpu.SMEM)
LIMIT = pltpu.CompilerParams(vmem_limit_bytes=44 * 2**20)


def cost(flops, *arrays):
    touched = sum(array.size * array.dtype.itemsize for array in arrays)
    return pl.CostEstimate(flops=flops, bytes_accessed=2 * touched, transcendentals=0)


def stack_pieces(places, rows, pieces, whole):
    me = lax.axis_index("real")
    for (distance, row), piece in zip(places, pieces):
        height = piece.shape[0]
        start = pl.multiple_of((me ^ distance) * rows + row, height)
        whole[pl.ds(start, height), :] = piece[...]


def project_columns(v_columns, noise_ref):
    projected = lax.dot_general(
        v_columns, noise_ref[...], (((0,), (0,)), ((), ())), preferred_element_type=jnp.float32
    )
    return projected.astype(jnp.bfloat16)


def project_kernel(places, rows, noise_ref, *refs):
    pieces, outs, whole = refs[: len(places)], refs[len(places) : -1], refs[-1]
    stack_pieces(places, rows, pieces, whole)
    for place, out_ref in enumerate(outs):
        columns = out_ref.shape[0]
        out_ref[...] = project_columns(
            whole[:, place * columns : (place + 1) * columns], noise_ref
        )


def project(n_shifts, noise, gathered):
    sites, reals = noise.shape
    places, pieces = zip(*gathered)
    rows, columns = pieces[0].shape
    return pl.pallas_call(
        functools.partial(project_kernel, places, rows),
        out_shape=[jax.ShapeDtypeStruct((columns // n_shifts, reals), jnp.bfloat16)] * n_shifts,
        in_specs=[VMEM] * (1 + len(pieces)),
        out_specs=[VMEM] * n_shifts,
        scratch_shapes=[pltpu.VMEM((sites, columns), jnp.bfloat16)],
        compiler_params=LIMIT,
        cost_estimate=cost(2 * sites * columns * reals, noise, *pieces),
        name=f"project_{n_shifts}",
    )(noise, *pieces)


def stage_kernel(from_ref, to_ref, sems):
    parts = sems.shape[0]
    rows = from_ref.shape[0] // parts
    copies = []
    for part in range(parts):
        span = slice(part * rows, (part + 1) * rows)
        copies.append(
            pltpu.make_async_copy(from_ref.at[span, :], to_ref.at[span, :], sems.at[part])
        )
        copies[-1].start()
    for copy in copies:
        copy.wait()


def stage(array):
    return pl.pallas_call(
        stage_kernel,
        out_shape=jax.ShapeDtypeStruct(array.shape, array.dtype),
        in_specs=[pl.BlockSpec(memory_space=pltpu.HBM)],
        out_specs=VMEM,
        scratch_shapes=[pltpu.SemaphoreType.DMA((4,))],
        compiler_params=LIMIT,
        cost_estimate=cost(0, array),
        name="stage",
    )(array)


def source_of(shift):
    site_count = lax.axis_size("site")
    return lax.rem(lax.axis_index("site") + (site_count - shift), site_count)


def alive_coef(shift, ranks_ref, coef):
    rank = ranks_ref[lax.axis_index("site"), source_of(shift)]
    row = lax.broadcasted_iota(jnp.int32, coef.shape, 0)
    alive = row < rank * (coef.shape[0] // CAP)
    return jnp.where(alive, coef.astype(jnp.float32), 0.0).astype(coef.dtype)


def accumulate_kernel(shifts, places, rows, ranks_ref, *refs):
    pieces, coefs = refs[: len(places)], refs[len(places) : len(places) + len(shifts)]
    u_ref, sum_ref = refs[-2:]
    stack_pieces(places, rows, pieces, u_ref)
    total = jnp.zeros(sum_ref.shape, jnp.float32)
    for shift, coef_ref in zip(shifts, coefs):
        per_source = coef_ref.shape[0]
        start = pl.multiple_of(source_of(shift) * per_source, per_source)
        total += jnp.dot(
            u_ref[:, pl.ds(start, per_source)],
            alive_coef(shift, ranks_ref, coef_ref[...]),
            preferred_element_type=jnp.float32,
        )
    sum_ref[...] = total


def accumulate(shifts, ranks, gathered, coefs):
    places, pieces = zip(*gathered)
    rows, columns = pieces[0].shape
    sites = rows * lax.axis_size("real")
    per_source, reals = coefs[0].shape
    return pl.pallas_call(
        functools.partial(accumulate_kernel, shifts, places, rows),
        out_shape=[
            jax.ShapeDtypeStruct((sites, columns), jnp.bfloat16),
            jax.ShapeDtypeStruct((sites, reals), jnp.float32),
        ],
        in_specs=[SMEM] + [VMEM] * (len(pieces) + len(coefs)),
        out_specs=[VMEM] * 2,
        compiler_params=LIMIT,
        cost_estimate=cost(2 * sites * len(coefs) * per_source * reals, *pieces, *coefs),
        name="accumulate",
    )(ranks, *pieces, *coefs)


def finish_kernel(shifts, ranks_ref, u_ref, sum_ref, skew_ref, tail_ref, *refs):
    coefs = refs[: len(shifts)]
    out_ref, slots, sems = refs[len(shifts) :]
    block = slots.shape[1]
    alive = [alive_coef(shift, ranks_ref, coef[...]) for shift, coef in zip(shifts, coefs)]
    copies = []
    for step in range(out_ref.shape[0] // block):
        rows = slice(step * block, (step + 1) * block)
        gaussian = sum_ref[rows, :]
        for shift, coef in zip(shifts, alive):
            columns = coef.shape[0]
            start = pl.multiple_of(source_of(shift) * columns, columns)
            gaussian += jnp.dot(
                u_ref[rows, pl.ds(start, columns)], coef, preferred_element_type=jnp.float32
            )
        skew, tail = skew_ref[rows, :], tail_ref[rows, :]
        grown = jnp.exp2((skew * LOG2E) * gaussian) + 1.0
        grown = grown * jnp.tanh((0.5 * skew) * gaussian) * (1.0 / skew)
        slots[step] = grown * jnp.exp2((0.5 * LOG2E * tail) * (gaussian * gaussian))
        copy = pltpu.make_async_copy(slots.at[step], out_ref.at[rows, :], sems.at[step])
        copy.start()
        copies.append(copy)
    for copy in copies:
        copy.wait()


def finish(shifts, ranks, u_whole, total, skew, tail, coefs):
    rows, columns = u_whole.shape
    per_source, reals = coefs[0].shape
    block = min(rows, 128)
    return pl.pallas_call(
        functools.partial(finish_kernel, shifts),
        out_shape=jax.ShapeDtypeStruct((rows, reals), jnp.float32),
        in_specs=[SMEM] + [VMEM] * (4 + len(coefs)),
        out_specs=pl.BlockSpec(memory_space=pl.ANY),
        scratch_shapes=[
            pltpu.VMEM((rows // block, block, reals), jnp.float32),
            pltpu.SemaphoreType.DMA((rows // block,)),
        ],
        compiler_params=LIMIT,
        cost_estimate=cost(2 * rows * len(coefs) * per_source * reals, u_whole, total, *coefs),
        name="finish",
    )(ranks, u_whole, total, skew, tail, *coefs)


def after(value, *before):
    return lax.optimization_barrier((value, before))[0]


def swap(array, distance):
    count = lax.axis_size("real")
    return lax.ppermute(array, "real", [(k, k ^ distance) for k in range(count)])


def with_other_core(pieces):
    both = dict(pieces)
    for (distance, row), piece in pieces.items():
        if (distance ^ 1, row) not in pieces:
            both[distance ^ 1, row] = swap(piece, 1)
    return both


def from_chips(own):
    pieces = {(0, 0): own}
    for distance in range(2, lax.axis_size("real"), 2):
        pieces[distance, 0] = swap(own, distance)
    return pieces


def two_at_a_time(own):
    distances = range(2, lax.axis_size("real"), 2)
    pieces, tails = {(0, 0): own}, [own, own]
    for turn, distance in enumerate(distances):
        tails[turn % 2] = pieces[distance, 0] = swap(after(own, tails[turn % 2]), distance)
    last, tail = distances[-1], tails[len(distances) % 2]
    for distance in (0, *distances[:-1]):
        tail = pieces[distance ^ 1, 0] = swap(after(pieces[distance, 0], tail), 1)
    pieces[last ^ 1, 0] = swap(pieces[last, 0], 1)
    return pieces


def at_once(present, gather, pieces):
    places, arrays, new = list(pieces), list(pieces.values()), []

    def added(*arrays):
        more = gather(dict(zip(places, arrays)))
        new[:] = [place for place in more if place not in pieces]
        return [more[place] for place in new]

    count = len(jax.eval_shape(added, *arrays))
    results = lax.cond(present, added, lambda *same: [same[0]] * count, *arrays)
    return {**pieces, **dict(zip(new, results))}


def along_site(coef, shift):
    count = lax.axis_size("site")
    return lax.ppermute(coef, "site", [(k, (k + shift) % count) for k in range(count)])


def per_device(noise, v_factors, u_factors, ranks, skew_g, tail_h):
    site_count = lax.axis_size("site")
    real_count = lax.axis_size("real")
    source = lax.axis_index("site")
    rows, columns = v_factors.shape[1:]
    per_dest = columns // site_count
    middle = site_count // 2
    others = sorted(range(1, site_count), key=lambda shift: (abs(shift - middle), shift))
    first, rest = others[0], tuple(others[1:])

    def columns_for(shift):
        start = lax.rem(source + shift, site_count) * per_dest
        return lax.dynamic_slice(v_factors[0], (0, start), (rows, per_dest))

    v_first = columns_for(first)
    v_rest = jnp.concatenate([columns_for(shift) for shift in rest + (0,)], axis=1)
    present = ranks[0, 0] > 0
    v_first = from_chips(v_first)
    last = max(v_first)
    waiting = (v_first[last], stage(noise), v_rest, present)
    v_first[last], noise, v_rest, present = lax.optimization_barrier(waiting)
    v_first = with_other_core(v_first)
    v_rest = from_chips(after(v_rest, *v_first.values()))
    [far] = project(1, noise, v_first.items())

    v_rest = at_once(present, with_other_core, after(v_rest, far))
    *others, own = project(len(rest) + 1, noise, v_rest.items())
    far = along_site(far, first)
    others = [along_site(coef, shift) for coef, shift in zip(others, rest)]

    u_pieces = at_once(
        present, lambda pieces: two_at_a_time(pieces[0, 0]), {(0, 0): after(u_factors[0], own)}
    )
    u_whole, total = accumulate((0, first), ranks, u_pieces.items(), [own, far])
    return finish(rest, ranks, u_whole, total, skew_g[:, None], tail_h[:, None], others)


def solution(mesh):
    placed = (
        P("site", "real"),
        P("site", "real", None),
        P("site", "real", None),
        P(),
        P("site"),
        P("site"),
    )
    return jax.shard_map(
        per_device, mesh=mesh, in_specs=placed, out_specs=P("site", "real"), check_vma=False
    )
```

```python
import functools

import jax
import jax.numpy as jnp
from jax import lax
from jax.experimental import pallas as pl
from jax.experimental.pallas import tpu as pltpu
from jax.sharding import PartitionSpec as P

CAP = 2
LOG2E = 1.4426950408889634
VMEM = pl.BlockSpec(memory_space=pltpu.VMEM)
SMEM = pl.BlockSpec(memory_space=pltpu.SMEM)
LIMIT = pltpu.CompilerParams(vmem_limit_bytes=44 * 2**20)


def cost(flops, *arrays):
    touched = sum(array.size * array.dtype.itemsize for array in arrays)
    return pl.CostEstimate(flops=flops, bytes_accessed=2 * touched, transcendentals=0)


def stack_pieces(places, rows, pieces, whole):
    me = lax.axis_index("real")
    for (distance, row), piece in zip(places, pieces):
        height = piece.shape[0]
        start = pl.multiple_of((me ^ distance) * rows + row, height)
        whole[pl.ds(start, height), :] = piece[...]


def project_columns(v_columns, noise_ref):
    projected = lax.dot_general(
        v_columns, noise_ref[...], (((0,), (0,)), ((), ())), preferred_element_type=jnp.float32
    )
    return projected.astype(jnp.bfloat16)


def project_kernel(places, rows, noise_ref, *refs):
    pieces, outs, whole = refs[: len(places)], refs[len(places) : -1], refs[-1]
    stack_pieces(places, rows, pieces, whole)
    for place, out_ref in enumerate(outs):
        columns = out_ref.shape[0]
        out_ref[...] = project_columns(
            whole[:, place * columns : (place + 1) * columns], noise_ref
        )


def project(n_shifts, noise, gathered):
    sites, reals = noise.shape
    places, pieces = zip(*gathered)
    rows, columns = pieces[0].shape
    return pl.pallas_call(
        functools.partial(project_kernel, places, rows),
        out_shape=[jax.ShapeDtypeStruct((columns // n_shifts, reals), jnp.bfloat16)] * n_shifts,
        in_specs=[VMEM] * (1 + len(pieces)),
        out_specs=[VMEM] * n_shifts,
        scratch_shapes=[pltpu.VMEM((sites, columns), jnp.bfloat16)],
        compiler_params=LIMIT,
        cost_estimate=cost(2 * sites * columns * reals, noise, *pieces),
        name=f"project_{n_shifts}",
    )(noise, *pieces)


def stage_kernel(from_ref, to_ref, sems):
    parts = sems.shape[0]
    rows = from_ref.shape[0] // parts
    copies = []
    for part in range(parts):
        span = slice(part * rows, (part + 1) * rows)
        copies.append(
            pltpu.make_async_copy(from_ref.at[span, :], to_ref.at[span, :], sems.at[part])
        )
        copies[-1].start()
    for copy in copies:
        copy.wait()


def stage(array):
    return pl.pallas_call(
        stage_kernel,
        out_shape=jax.ShapeDtypeStruct(array.shape, array.dtype),
        in_specs=[pl.BlockSpec(memory_space=pltpu.HBM)],
        out_specs=VMEM,
        scratch_shapes=[pltpu.SemaphoreType.DMA((4,))],
        compiler_params=LIMIT,
        cost_estimate=cost(0, array),
        name="stage",
    )(array)


def source_of(shift):
    site_count = lax.axis_size("site")
    return lax.rem(lax.axis_index("site") + (site_count - shift), site_count)


def alive_coef(shift, ranks_ref, coef):
    rank = ranks_ref[lax.axis_index("site"), source_of(shift)]
    row = lax.broadcasted_iota(jnp.int32, coef.shape, 0)
    alive = row < rank * (coef.shape[0] // CAP)
    return jnp.where(alive, coef.astype(jnp.float32), 0.0).astype(coef.dtype)


def accumulate_kernel(shifts, places, rows, ranks_ref, noise_ref, *refs):
    pieces, coefs = refs[: len(places)], refs[len(places) : len(places) + len(shifts)]
    u_ref, sum_ref, whole = refs[-3:]
    stack_pieces(places, rows, pieces, whole)
    per_source = whole.shape[1] - u_ref.shape[1]
    u_ref[...] = whole[:, per_source:]
    own = project_columns(whole[:, :per_source], noise_ref)
    total = jnp.zeros(sum_ref.shape, jnp.float32)
    for shift, coef in zip((0,) + shifts, [own] + [coef_ref[...] for coef_ref in coefs]):
        start = pl.multiple_of(source_of(shift) * per_source, per_source)
        total += jnp.dot(
            u_ref[:, pl.ds(start, per_source)],
            alive_coef(shift, ranks_ref, coef),
            preferred_element_type=jnp.float32,
        )
    sum_ref[...] = total


def accumulate(shifts, ranks, noise, gathered, coefs):
    places, pieces = zip(*gathered)
    rows, columns = pieces[0].shape
    sites, reals = noise.shape
    per_source = coefs[0].shape[0]
    return pl.pallas_call(
        functools.partial(accumulate_kernel, shifts, places, rows),
        out_shape=[
            jax.ShapeDtypeStruct((sites, columns - per_source), jnp.bfloat16),
            jax.ShapeDtypeStruct((sites, reals), jnp.float32),
        ],
        in_specs=[SMEM] + [VMEM] * (1 + len(pieces) + len(coefs)),
        out_specs=[VMEM] * 2,
        scratch_shapes=[pltpu.VMEM((sites, columns), jnp.bfloat16)],
        compiler_params=LIMIT,
        cost_estimate=cost(6 * sites * per_source * reals, noise, *pieces, *coefs),
        name="accumulate",
    )(ranks, noise, *pieces, *coefs)


def finish_kernel(shifts, ranks_ref, u_ref, sum_ref, skew_ref, tail_ref, *refs):
    coefs = refs[: len(shifts)]
    out_ref, slots, sems = refs[len(shifts) :]
    block = slots.shape[1]
    alive = [alive_coef(shift, ranks_ref, coef[...]) for shift, coef in zip(shifts, coefs)]
    copies = []
    for step in range(out_ref.shape[0] // block):
        rows = slice(step * block, (step + 1) * block)
        gaussian = sum_ref[rows, :]
        for shift, coef in zip(shifts, alive):
            columns = coef.shape[0]
            start = pl.multiple_of(source_of(shift) * columns, columns)
            gaussian += jnp.dot(
                u_ref[rows, pl.ds(start, columns)], coef, preferred_element_type=jnp.float32
            )
        skew, tail = skew_ref[rows, :], tail_ref[rows, :]
        grown = jnp.exp2((skew * LOG2E) * gaussian) + 1.0
        grown = grown * jnp.tanh((0.5 * skew) * gaussian) * (1.0 / skew)
        slots[step] = grown * jnp.exp2((0.5 * LOG2E * tail) * (gaussian * gaussian))
        copy = pltpu.make_async_copy(slots.at[step], out_ref.at[rows, :], sems.at[step])
        copy.start()
        copies.append(copy)
    for copy in copies:
        copy.wait()


def finish(shifts, ranks, u_whole, total, skew, tail, coefs):
    rows, columns = u_whole.shape
    per_source, reals = coefs[0].shape
    block = min(rows, 128)
    return pl.pallas_call(
        functools.partial(finish_kernel, shifts),
        out_shape=jax.ShapeDtypeStruct((rows, reals), jnp.float32),
        in_specs=[SMEM] + [VMEM] * (4 + len(coefs)),
        out_specs=pl.BlockSpec(memory_space=pl.ANY),
        scratch_shapes=[
            pltpu.VMEM((rows // block, block, reals), jnp.float32),
            pltpu.SemaphoreType.DMA((rows // block,)),
        ],
        compiler_params=LIMIT,
        cost_estimate=cost(2 * rows * len(coefs) * per_source * reals, u_whole, total, *coefs),
        name="finish",
    )(ranks, u_whole, total, skew, tail, *coefs)


def after(value, *before):
    return lax.optimization_barrier((value, before))[0]


def swap(array, distance):
    count = lax.axis_size("real")
    return lax.ppermute(array, "real", [(k, k ^ distance) for k in range(count)])


def with_other_core(pieces):
    both = dict(pieces)
    for (distance, row), piece in pieces.items():
        if (distance ^ 1, row) not in pieces:
            both[distance ^ 1, row] = swap(piece, 1)
    return both


def from_chips(own):
    pieces = {(0, 0): own}
    for distance in range(2, lax.axis_size("real"), 2):
        pieces[distance, 0] = swap(own, distance)
    return pieces


def neighbour_distances():
    return (2, 4) if lax.axis_size("real") == 8 else ()


def chunk_and_neighbours(chunk, later):
    pieces, tail = from_chips(chunk), chunk
    for distance, _ in list(pieces):
        tail = pieces[distance ^ 1, 0] = swap(after(pieces[distance, 0], tail), 1)
    near = {}
    for distance in neighbour_distances():
        near[distance, 0] = swap(after(later, pieces[distance, 0]), distance)
    return {place: pieces[place] for place in pieces if place != (0, 0)}, near


def two_at_a_time(pieces):
    known, pieces = pieces, dict(pieces)
    own = pieces[0, 0]
    distances = [d for d in range(2, lax.axis_size("real"), 2) if (d, 0) not in pieces]
    tails = [own, own]
    for turn, distance in enumerate(distances):
        tails[turn % 2] = pieces[distance, 0] = swap(after(own, tails[turn % 2]), distance)
    last, tail = distances[-1], tails[len(distances) % 2]
    for distance in range(0, lax.axis_size("real"), 2):
        if distance != last:
            tail = pieces[distance ^ 1, 0] = swap(after(pieces[distance, 0], tail), 1)
    pieces[last ^ 1, 0] = swap(pieces[last, 0], 1)
    return {place: pieces[place] for place in pieces if place not in known}


def at_once(present, gather, *args):
    shapes, tree = [], []

    def flat(*args):
        leaves, structure = jax.tree.flatten(gather(*args))
        tree[:] = [structure]
        return leaves

    shapes = jax.eval_shape(flat, *args)
    nothing = lambda *_: [jnp.zeros(leaf.shape, leaf.dtype) for leaf in shapes]
    return jax.tree.unflatten(tree[0], lax.cond(present, flat, nothing, *args))


def along_site(coef, shift):
    count = lax.axis_size("site")
    return lax.ppermute(coef, "site", [(k, (k + shift) % count) for k in range(count)])


def per_device(noise, v_factors, u_factors, ranks, skew_g, tail_h):
    site_count = lax.axis_size("site")
    real_count = lax.axis_size("real")
    source = lax.axis_index("site")
    rows, columns = v_factors.shape[1:]
    per_dest = columns // site_count
    middle = site_count // 2
    others = sorted(range(1, site_count), key=lambda shift: (abs(shift - middle), shift))
    first, rest = others[0], tuple(others[1:])

    def columns_for(shift):
        start = lax.rem(source + shift, site_count) * per_dest
        return lax.dynamic_slice(v_factors[0], (0, start), (rows, per_dest))

    v_first = columns_for(first)
    v_rest = jnp.concatenate([columns_for(shift) for shift in rest], axis=1)
    own_and_u = jnp.concatenate([columns_for(0), u_factors[0]], axis=1)
    v_first = from_chips(v_first)
    last = max(v_first)
    waiting = (v_first[last], stage(noise), v_rest, own_and_u)
    v_first[last], noise, v_rest, own_and_u = lax.optimization_barrier(waiting)
    present = ranks[0, 0] > 0
    [far] = project(1, noise, with_other_core(v_first).items())
    v_rest = after(v_rest, far)
    v_pieces, u_pieces = at_once(present, chunk_and_neighbours, v_rest, own_and_u)
    others = project(len(rest), noise, {(0, 0): v_rest, **v_pieces}.items())
    far = along_site(far, first)
    u_pieces = after({(0, 0): own_and_u, **u_pieces}, others[0])
    u_pieces.update(at_once(present, two_at_a_time, u_pieces))
    others = [along_site(coef, shift) for coef, shift in zip(others, rest)]
    u_whole, total = accumulate((first,), ranks, noise, u_pieces.items(), [far])
    return finish(rest, ranks, u_whole, total, skew_g[:, None], tail_h[:, None], others)


def solution(mesh):
    placed = (
        P("site", "real"),
        P("site", "real", None),
        P("site", "real", None),
        P(),
        P("site"),
        P("site"),
    )
    return jax.shard_map(
        per_device, mesh=mesh, in_specs=placed, out_specs=P("site", "real"), check_vma=False
    )
```

```python
import functools
import math

import jax
import jax.numpy as jnp
from jax import lax
from jax.experimental import pallas as pl
from jax.experimental.pallas import tpu as pltpu
from jax.sharding import PartitionSpec as P

CAP = 2
LOG2E = 1.4426950408889634
VMEM = pl.BlockSpec(memory_space=pltpu.VMEM)
SMEM = pl.BlockSpec(memory_space=pltpu.SMEM)


def vmem(*shapes):
    held = sum(4 * math.prod(shape) for shape in shapes)
    return pltpu.CompilerParams(vmem_limit_bytes=held + 6 * 2**20)


def cost(flops, *arrays):
    touched = sum(array.size * array.dtype.itemsize for array in arrays)
    return pl.CostEstimate(flops=flops, bytes_accessed=2 * touched, transcendentals=0)


def stack_pieces(places, rows, pieces, whole):
    me = lax.axis_index("real")
    for (distance, row), piece in zip(places, pieces):
        height = piece.shape[0]
        start = pl.multiple_of((me ^ distance) * rows + row, height)
        whole[pl.ds(start, height), :] = piece[...]


def project_columns(v_columns, noise_ref):
    projected = lax.dot_general(
        v_columns, noise_ref[...], (((0,), (0,)), ((), ())), preferred_element_type=jnp.float32
    )
    return projected.astype(jnp.bfloat16)


def project_kernel(places, rows, noise_ref, *refs):
    pieces, outs, whole = refs[: len(places)], refs[len(places) : -1], refs[-1]
    stack_pieces(places, rows, pieces, whole)
    for place, out_ref in enumerate(outs):
        columns = out_ref.shape[0]
        out_ref[...] = project_columns(
            whole[:, place * columns : (place + 1) * columns], noise_ref
        )


def project(n_shifts, noise, gathered):
    sites, reals = noise.shape
    places, pieces = zip(*gathered)
    rows, columns = pieces[0].shape
    return pl.pallas_call(
        functools.partial(project_kernel, places, rows),
        out_shape=[jax.ShapeDtypeStruct((columns // n_shifts, reals), jnp.bfloat16)] * n_shifts,
        in_specs=[VMEM] * (1 + len(pieces)),
        out_specs=[VMEM] * n_shifts,
        scratch_shapes=[pltpu.VMEM((sites, columns), jnp.bfloat16)],
        compiler_params=vmem(noise.shape, (sites, 2 * columns)),
        cost_estimate=cost(2 * sites * columns * reals, noise, *pieces),
        name=f"project_{n_shifts}",
    )(noise, *pieces)


def stage_kernel(from_ref, to_ref, sems):
    parts = sems.shape[0]
    rows = from_ref.shape[0] // parts
    copies = []
    for part in range(parts):
        span = slice(part * rows, (part + 1) * rows)
        copies.append(
            pltpu.make_async_copy(from_ref.at[span, :], to_ref.at[span, :], sems.at[part])
        )
        copies[-1].start()
    for copy in copies:
        copy.wait()


def stage(array):
    return pl.pallas_call(
        stage_kernel,
        out_shape=jax.ShapeDtypeStruct(array.shape, array.dtype),
        in_specs=[pl.BlockSpec(memory_space=pltpu.HBM)],
        out_specs=VMEM,
        scratch_shapes=[pltpu.SemaphoreType.DMA((4,))],
        compiler_params=vmem(array.shape),
        cost_estimate=cost(0, array),
        name="stage",
    )(array)


def source_of(shift):
    site_count = lax.axis_size("site")
    return lax.rem(lax.axis_index("site") + (site_count - shift), site_count)


def alive_coef(shift, ranks_ref, coef):
    rank = ranks_ref[lax.axis_index("site"), source_of(shift)]
    row = lax.broadcasted_iota(jnp.int32, coef.shape, 0)
    alive = row < rank * (coef.shape[0] // CAP)
    return jnp.where(alive, coef.astype(jnp.float32), 0.0).astype(coef.dtype)


def accumulate_kernel(shifts, places, rows, ranks_ref, noise_ref, *refs):
    pieces, coefs = refs[: len(places)], refs[len(places) : len(places) + len(shifts)]
    u_ref, sum_ref, whole = refs[-3:]
    stack_pieces(places, rows, pieces, whole)
    per_source = whole.shape[1] - u_ref.shape[1]
    u_ref[...] = whole[:, per_source:]
    own = project_columns(whole[:, :per_source], noise_ref)
    total = jnp.zeros(sum_ref.shape, jnp.float32)
    for shift, coef in zip((0,) + shifts, [own] + [coef_ref[...] for coef_ref in coefs]):
        start = pl.multiple_of(source_of(shift) * per_source, per_source)
        total += jnp.dot(
            u_ref[:, pl.ds(start, per_source)],
            alive_coef(shift, ranks_ref, coef),
            preferred_element_type=jnp.float32,
        )
    sum_ref[...] = total


def accumulate(shifts, ranks, noise, gathered, coefs):
    places, pieces = zip(*gathered)
    sites, reals = noise.shape
    rows, columns = sites // lax.axis_size("real"), pieces[0].shape[1]
    per_source = coefs[0].shape[0]
    return pl.pallas_call(
        functools.partial(accumulate_kernel, shifts, places, rows),
        out_shape=[
            jax.ShapeDtypeStruct((sites, columns - per_source), jnp.bfloat16),
            jax.ShapeDtypeStruct((sites, reals), jnp.float32),
        ],
        in_specs=[SMEM] + [VMEM] * (1 + len(pieces) + len(coefs)),
        out_specs=[VMEM] * 2,
        scratch_shapes=[pltpu.VMEM((sites, columns), jnp.bfloat16)],
        compiler_params=vmem((sites, 3 * reals), (sites, 2 * columns)),
        cost_estimate=cost(6 * sites * per_source * reals, noise, *pieces, *coefs),
        name="accumulate",
    )(ranks, noise, *pieces, *coefs)


def finish_kernel(shifts, ranks_ref, u_ref, sum_ref, skew_ref, tail_ref, *refs):
    coefs = refs[: len(shifts)]
    out_ref, slots, sems = refs[len(shifts) :]
    block = slots.shape[1]
    alive = [alive_coef(shift, ranks_ref, coef[...]) for shift, coef in zip(shifts, coefs)]
    copies = []
    for step in range(out_ref.shape[0] // block):
        rows = slice(step * block, (step + 1) * block)
        gaussian = sum_ref[rows, :]
        for shift, coef in zip(shifts, alive):
            columns = coef.shape[0]
            start = pl.multiple_of(source_of(shift) * columns, columns)
            gaussian += jnp.dot(
                u_ref[rows, pl.ds(start, columns)], coef, preferred_element_type=jnp.float32
            )
        skew, tail = skew_ref[rows, :], tail_ref[rows, :]
        grown = jnp.exp2((skew * LOG2E) * gaussian) + 1.0
        grown = grown * jnp.tanh((0.5 * skew) * gaussian) * (1.0 / skew)
        slots[step] = grown * jnp.exp2((0.5 * LOG2E * tail) * (gaussian * gaussian))
        copy = pltpu.make_async_copy(slots.at[step], out_ref.at[rows, :], sems.at[step])
        copy.start()
        copies.append(copy)
    for copy in copies:
        copy.wait()


def finish(shifts, ranks, u_whole, total, skew, tail, coefs):
    rows, columns = u_whole.shape
    per_source, reals = coefs[0].shape
    block = min(rows, 128)
    return pl.pallas_call(
        functools.partial(finish_kernel, shifts),
        out_shape=jax.ShapeDtypeStruct((rows, reals), jnp.float32),
        in_specs=[SMEM] + [VMEM] * (4 + len(coefs)),
        out_specs=pl.BlockSpec(memory_space=pl.ANY),
        scratch_shapes=[
            pltpu.VMEM((rows // block, block, reals), jnp.float32),
            pltpu.SemaphoreType.DMA((rows // block,)),
        ],
        compiler_params=vmem((rows, 4 * reals), u_whole.shape),
        cost_estimate=cost(2 * rows * len(coefs) * per_source * reals, u_whole, total, *coefs),
        name="finish",
    )(ranks, u_whole, total, skew, tail, *coefs)


def after(value, *before):
    return lax.optimization_barrier((value, before))[0]


def swap(array, distance):
    count = lax.axis_size("real")
    return lax.ppermute(array, "real", [(k, k ^ distance) for k in range(count)])


def with_other_core(pieces):
    both = dict(pieces)
    for (distance, row), piece in pieces.items():
        if (distance ^ 1, row) not in pieces:
            both[distance ^ 1, row] = swap(piece, 1)
    return both


def from_chips(own):
    pieces = {(0, 0): own}
    for distance in range(2, lax.axis_size("real"), 2):
        pieces[distance, 0] = swap(own, distance)
    return pieces


def neighbour_distances():
    return (2, 4) if lax.axis_size("real") == 8 else ()


def direct_rest(chunk):
    pieces = with_other_core(from_chips(chunk))
    del pieces[0, 0]
    return pieces


def relayed_rest(pieces):
    if (2, 0) not in pieces:
        return two_at_a_time(pieces)
    first, second = pieces[2, 0], pieces[4, 0]
    half = first.shape[0] // 2
    one, two = swap(second[:half], 2), swap(first[half:], 4)
    more = {(6, 0): one, (6, half): two}
    more[3, 0], more[5, 0] = swap(after(first, one), 1), swap(after(second, two), 1)
    more[7, 0], more[7, half] = swap(after(one, more[3, 0]), 1), swap(after(two, more[5, 0]), 1)
    return more


def two_at_a_time(pieces):
    known, pieces = pieces, dict(pieces)
    own = pieces[0, 0]
    distances = range(2, lax.axis_size("real"), 2)
    tails = [own, own]
    for turn, distance in enumerate(distances):
        tails[turn % 2] = pieces[distance, 0] = swap(after(own, tails[turn % 2]), distance)
    last, tail = distances[-1], tails[len(distances) % 2]
    for distance in (0, *distances):
        if distance != last and (distance ^ 1, 0) not in known:
            tail = pieces[distance ^ 1, 0] = swap(after(pieces[distance, 0], tail), 1)
    pieces[last ^ 1, 0] = swap(pieces[last, 0], 1)
    return {place: pieces[place] for place in pieces if place not in known}


def at_once(present, gather, *args):
    shapes, tree = [], []

    def flat(*args):
        leaves, structure = jax.tree.flatten(gather(*args))
        tree[:] = [structure]
        return leaves

    shapes = jax.eval_shape(flat, *args)
    nothing = lambda *_: [jnp.zeros(leaf.shape, leaf.dtype) for leaf in shapes]
    return jax.tree.unflatten(tree[0], lax.cond(present, flat, nothing, *args))


def along_site(coef, shift):
    count = lax.axis_size("site")
    return lax.ppermute(coef, "site", [(k, (k + shift) % count) for k in range(count)])


def per_device(noise, v_factors, u_factors, ranks, skew_g, tail_h):
    site_count = lax.axis_size("site")
    real_count = lax.axis_size("real")
    source = lax.axis_index("site")
    rows, columns = v_factors.shape[1:]
    per_dest = columns // site_count
    middle = site_count // 2
    others = sorted(range(1, site_count), key=lambda shift: (abs(shift - middle), shift))
    first, rest = others[0], tuple(others[1:])

    def columns_for(shift):
        start = lax.rem(source + shift, site_count) * per_dest
        return lax.dynamic_slice(v_factors[0], (0, start), (rows, per_dest))

    v_first = columns_for(first)
    v_rest = jnp.concatenate([columns_for(shift) for shift in rest], axis=1)
    own_and_u = jnp.concatenate([columns_for(0), u_factors[0]], axis=1)
    v_first = from_chips(v_first)
    last = max(v_first)
    waiting = (v_first[last], stage(noise), v_rest, own_and_u)
    v_first[last], noise, v_rest, own_and_u = lax.optimization_barrier(waiting)
    present = ranks[0, 0] > 0
    [far] = project(1, noise, with_other_core(v_first).items())
    v_rest = after(v_rest, far)
    u_pieces = {(0, 0): own_and_u, (1, 0): swap(after(own_and_u, far), 1)}
    v_pieces = {(0, 0): after(v_rest, u_pieces[1, 0])}
    v_pieces.update(at_once(present, direct_rest, v_pieces[0, 0]))
    for distance in neighbour_distances():
        u_pieces[distance, 0] = swap(after(own_and_u, v_pieces), distance)
    others = project(len(rest), noise, v_pieces.items())
    far = along_site(far, first)
    u_pieces = after(u_pieces, others[0])
    u_pieces.update(at_once(present, relayed_rest, u_pieces))
    others = [along_site(coef, shift) for coef, shift in zip(others, rest)]
    u_whole, total = accumulate((first,), ranks, noise, u_pieces.items(), [far])
    return finish(rest, ranks, u_whole, total, skew_g[:, None], tail_h[:, None], others)


def solution(mesh):
    placed = (
        P("site", "real"),
        P("site", "real", None),
        P("site", "real", None),
        P(),
        P("site"),
        P("site"),
    )
    return jax.shard_map(
        per_device, mesh=mesh, in_specs=placed, out_specs=P("site", "real"), check_vma=False
    )
```

```python
import functools
import math

import jax
import jax.numpy as jnp
from jax import lax
from jax.experimental import pallas as pl
from jax.experimental.pallas import tpu as pltpu
from jax.sharding import PartitionSpec as P

CAP = 2
LOG2E = 1.4426950408889634
VMEM = pl.BlockSpec(memory_space=pltpu.VMEM)
SMEM = pl.BlockSpec(memory_space=pltpu.SMEM)


def vmem(*shapes):
    held = sum(4 * math.prod(shape) for shape in shapes)
    return pltpu.CompilerParams(vmem_limit_bytes=held + 6 * 2**20)


def cost(flops, *arrays):
    touched = sum(array.size * array.dtype.itemsize for array in arrays)
    return pl.CostEstimate(flops=flops, bytes_accessed=2 * touched, transcendentals=0)


def stack_pieces(places, rows, pieces, whole):
    me = lax.axis_index("real")
    for (distance, row), piece in zip(places, pieces):
        height = piece.shape[0]
        start = pl.multiple_of((me ^ distance) * rows + row, height)
        whole[pl.ds(start, height), :] = piece[...]


def project_columns(v_columns, noise_ref):
    projected = lax.dot_general(
        v_columns, noise_ref[...], (((0,), (0,)), ((), ())), preferred_element_type=jnp.float32
    )
    return projected.astype(jnp.bfloat16)


def project_kernel(places, rows, noise_ref, *refs):
    pieces, outs, whole = refs[: len(places)], refs[len(places) : -1], refs[-1]
    stack_pieces(places, rows, pieces, whole)
    for place, out_ref in enumerate(outs):
        columns = out_ref.shape[0]
        out_ref[...] = project_columns(
            whole[:, place * columns : (place + 1) * columns], noise_ref
        )


def project(n_shifts, noise, gathered):
    sites, reals = noise.shape
    places, pieces = zip(*gathered)
    rows, columns = pieces[0].shape
    return pl.pallas_call(
        functools.partial(project_kernel, places, rows),
        out_shape=[jax.ShapeDtypeStruct((columns // n_shifts, reals), jnp.bfloat16)] * n_shifts,
        in_specs=[VMEM] * (1 + len(pieces)),
        out_specs=[VMEM] * n_shifts,
        scratch_shapes=[pltpu.VMEM((sites, columns), jnp.bfloat16)],
        compiler_params=vmem(noise.shape, (sites, 2 * columns)),
        cost_estimate=cost(2 * sites * columns * reals, noise, *pieces),
        name=f"project_{n_shifts}",
    )(noise, *pieces)


def stage_kernel(from_ref, to_ref, sems):
    parts = sems.shape[0]
    rows = from_ref.shape[0] // parts
    copies = []
    for part in range(parts):
        span = slice(part * rows, (part + 1) * rows)
        copies.append(
            pltpu.make_async_copy(from_ref.at[span, :], to_ref.at[span, :], sems.at[part])
        )
        copies[-1].start()
    for copy in copies:
        copy.wait()


def stage(array):
    return pl.pallas_call(
        stage_kernel,
        out_shape=jax.ShapeDtypeStruct(array.shape, array.dtype),
        in_specs=[pl.BlockSpec(memory_space=pltpu.HBM)],
        out_specs=VMEM,
        scratch_shapes=[pltpu.SemaphoreType.DMA((4,))],
        compiler_params=vmem(array.shape),
        cost_estimate=cost(0, array),
        name="stage",
    )(array)


def source_of(shift):
    site_count = lax.axis_size("site")
    return lax.rem(lax.axis_index("site") + (site_count - shift), site_count)


def alive_coef(shift, ranks_ref, coef):
    rank = ranks_ref[lax.axis_index("site"), source_of(shift)]
    row = lax.broadcasted_iota(jnp.int32, coef.shape, 0)
    alive = row < rank * (coef.shape[0] // CAP)
    return jnp.where(alive, coef.astype(jnp.float32), 0.0).astype(coef.dtype)


def accumulate_kernel(shifts, places, rows, ranks_ref, noise_ref, *refs):
    pieces, coefs = refs[: len(places)], refs[len(places) : len(places) + len(shifts)]
    u_ref, sum_ref, whole = refs[-3:]
    stack_pieces(places, rows, pieces, whole)
    per_source = whole.shape[1] - u_ref.shape[1]
    u_ref[...] = whole[:, per_source:]
    own = project_columns(whole[:, :per_source], noise_ref)
    total = jnp.zeros(sum_ref.shape, jnp.float32)
    for shift, coef in zip((0,) + shifts, [own] + [coef_ref[...] for coef_ref in coefs]):
        start = pl.multiple_of(source_of(shift) * per_source, per_source)
        total += jnp.dot(
            u_ref[:, pl.ds(start, per_source)],
            alive_coef(shift, ranks_ref, coef),
            preferred_element_type=jnp.float32,
        )
    sum_ref[...] = total


def accumulate(shifts, ranks, noise, gathered, coefs):
    places, pieces = zip(*gathered)
    sites, reals = noise.shape
    rows, columns = sites // lax.axis_size("real"), pieces[0].shape[1]
    per_source = coefs[0].shape[0]
    return pl.pallas_call(
        functools.partial(accumulate_kernel, shifts, places, rows),
        out_shape=[
            jax.ShapeDtypeStruct((sites, columns - per_source), jnp.bfloat16),
            jax.ShapeDtypeStruct((sites, reals), jnp.float32),
        ],
        in_specs=[SMEM] + [VMEM] * (1 + len(pieces) + len(coefs)),
        out_specs=[VMEM] * 2,
        scratch_shapes=[pltpu.VMEM((sites, columns), jnp.bfloat16)],
        compiler_params=vmem((sites, 3 * reals), (sites, 2 * columns)),
        cost_estimate=cost(6 * sites * per_source * reals, noise, *pieces, *coefs),
        name="accumulate",
    )(ranks, noise, *pieces, *coefs)


def finish_kernel(shifts, ranks_ref, u_ref, sum_ref, skew_ref, tail_ref, *refs):
    coefs = refs[: len(shifts)]
    out_ref, slots, sems = refs[len(shifts) :]
    block = slots.shape[1]
    alive = [alive_coef(shift, ranks_ref, coef[...]) for shift, coef in zip(shifts, coefs)]
    copies = []
    for step in range(out_ref.shape[0] // block):
        rows = slice(step * block, (step + 1) * block)
        gaussian = sum_ref[rows, :]
        for shift, coef in zip(shifts, alive):
            columns = coef.shape[0]
            start = pl.multiple_of(source_of(shift) * columns, columns)
            gaussian += jnp.dot(
                u_ref[rows, pl.ds(start, columns)], coef, preferred_element_type=jnp.float32
            )
        skew, tail = skew_ref[rows, :], tail_ref[rows, :]
        grown = jnp.exp2((skew * LOG2E) * gaussian) + 1.0
        grown = grown * jnp.tanh((0.5 * skew) * gaussian) * (1.0 / skew)
        slots[step] = grown * jnp.exp2((0.5 * LOG2E * tail) * (gaussian * gaussian))
        copy = pltpu.make_async_copy(slots.at[step], out_ref.at[rows, :], sems.at[step])
        copy.start()
        copies.append(copy)
    for copy in copies:
        copy.wait()


def finish(shifts, ranks, u_whole, total, skew, tail, coefs):
    rows, columns = u_whole.shape
    per_source, reals = coefs[0].shape
    block = min(rows, 128)
    return pl.pallas_call(
        functools.partial(finish_kernel, shifts),
        out_shape=jax.ShapeDtypeStruct((rows, reals), jnp.float32),
        in_specs=[SMEM] + [VMEM] * (4 + len(coefs)),
        out_specs=pl.BlockSpec(memory_space=pl.ANY),
        scratch_shapes=[
            pltpu.VMEM((rows // block, block, reals), jnp.float32),
            pltpu.SemaphoreType.DMA((rows // block,)),
        ],
        compiler_params=vmem((rows, 4 * reals), u_whole.shape),
        cost_estimate=cost(2 * rows * len(coefs) * per_source * reals, u_whole, total, *coefs),
        name="finish",
    )(ranks, u_whole, total, skew, tail, *coefs)


def after(value, *before):
    return lax.optimization_barrier((value, before))[0]


def swap(array, distance):
    count = lax.axis_size("real")
    return lax.ppermute(array, "real", [(k, k ^ distance) for k in range(count)])


def with_other_core(pieces):
    both = dict(pieces)
    for (distance, row), piece in pieces.items():
        if (distance ^ 1, row) not in pieces:
            both[distance ^ 1, row] = swap(piece, 1)
    return both


def from_chips(own):
    pieces = {(0, 0): own}
    for distance in range(2, lax.axis_size("real"), 2):
        pieces[distance, 0] = swap(own, distance)
    return pieces


def direct_rest(chunk):
    pieces = with_other_core(from_chips(chunk))
    del pieces[0, 0]
    return pieces


def from_other_core(pieces):
    return {place: array for place, array in with_other_core(pieces).items() if place not in pieces}


def at_once(present, gather, *args):
    shapes, tree = [], []

    def flat(*args):
        leaves, structure = jax.tree.flatten(gather(*args))
        tree[:] = [structure]
        return leaves

    shapes = jax.eval_shape(flat, *args)
    nothing = lambda *_: [jnp.zeros(leaf.shape, leaf.dtype) for leaf in shapes]
    return jax.tree.unflatten(tree[0], lax.cond(present, flat, nothing, *args))


def along_site(coef, shift):
    count = lax.axis_size("site")
    return lax.ppermute(coef, "site", [(k, (k + shift) % count) for k in range(count)])


def per_device(noise, v_factors, u_factors, ranks, skew_g, tail_h):
    site_count = lax.axis_size("site")
    real_count = lax.axis_size("real")
    source = lax.axis_index("site")
    rows, columns = v_factors.shape[1:]
    per_dest = columns // site_count
    middle = site_count // 2
    others = sorted(range(1, site_count), key=lambda shift: (abs(shift - middle), shift))
    first, rest = others[0], tuple(others[1:])

    def columns_for(shift):
        start = lax.rem(source + shift, site_count) * per_dest
        return lax.dynamic_slice(v_factors[0], (0, start), (rows, per_dest))

    v_first = columns_for(first)
    v_rest = jnp.concatenate([columns_for(shift) for shift in rest], axis=1)
    own_and_u = jnp.concatenate([columns_for(0), u_factors[0]], axis=1)
    v_first = from_chips(v_first)
    last = max(v_first)
    waiting = (v_first[last], stage(noise), v_rest, own_and_u)
    v_first[last], noise_here, v_rest, own_and_u = lax.optimization_barrier(waiting)
    present = ranks[0, 0] > 0
    noise_here, present = lax.optimization_barrier((noise_here, present))
    [far] = project(1, noise_here, with_other_core(v_first).items())

    u_swapped = swap(after(own_and_u, far), 1)
    v_rest = after(v_rest, far, u_swapped)
    v_pieces = {(0, 0): v_rest, **at_once(present, direct_rest, v_rest)}
    u_pieces = from_chips(after(own_and_u, v_pieces))
    others = project(len(rest), noise_here, v_pieces.items())
    far = along_site(far, first)
    others = after(others, far)
    u_pieces = {**u_pieces, (1, 0): u_swapped}
    u_pieces.update(at_once(present, from_other_core, u_pieces))
    others = [along_site(coef, shift) for coef, shift in zip(others, rest)]
    u_whole, total = accumulate((first,), ranks, noise, u_pieces.items(), [far])
    return finish(rest, ranks, u_whole, total, skew_g[:, None], tail_h[:, None], others)


def solution(mesh):
    placed = (
        P("site", "real"),
        P("site", "real", None),
        P("site", "real", None),
        P(),
        P("site"),
        P("site"),
    )
    return jax.shard_map(
        per_device, mesh=mesh, in_specs=placed, out_specs=P("site", "real"), check_vma=False
    )
```

```python
import functools
import math

import jax
import jax.numpy as jnp
from jax import lax
from jax.experimental import pallas as pl
from jax.experimental.pallas import tpu as pltpu
from jax.sharding import PartitionSpec as P

CAP = 2
LOG2E = 1.4426950408889634
VMEM = pl.BlockSpec(memory_space=pltpu.VMEM)
SMEM = pl.BlockSpec(memory_space=pltpu.SMEM)


def vmem(*shapes):
    held = sum(4 * math.prod(shape) for shape in shapes)
    return pltpu.CompilerParams(vmem_limit_bytes=held + 6 * 2**20)


def cost(flops, *arrays):
    touched = sum(array.size * array.dtype.itemsize for array in arrays)
    return pl.CostEstimate(flops=flops, bytes_accessed=2 * touched, transcendentals=0)


def stack_pieces(places, rows, pieces, whole):
    me = lax.axis_index("real")
    for (distance, row), piece in zip(places, pieces):
        height = piece.shape[0]
        start = pl.multiple_of((me ^ distance) * rows + row, height)
        whole[pl.ds(start, height), :] = piece[...]


def project_columns(v_columns, noise_ref):
    projected = lax.dot_general(
        v_columns, noise_ref[...], (((0,), (0,)), ((), ())), preferred_element_type=jnp.float32
    )
    return projected.astype(jnp.bfloat16)


def project_kernel(places, rows, noise_ref, *refs):
    pieces, outs, whole = refs[: len(places)], refs[len(places) : -1], refs[-1]
    stack_pieces(places, rows, pieces, whole)
    for place, out_ref in enumerate(outs):
        columns = out_ref.shape[0]
        out_ref[...] = project_columns(
            whole[:, place * columns : (place + 1) * columns], noise_ref
        )


def project(n_shifts, noise, gathered):
    sites, reals = noise.shape
    places, pieces = zip(*gathered)
    rows, columns = pieces[0].shape
    return pl.pallas_call(
        functools.partial(project_kernel, places, rows),
        out_shape=[pltpu.VMEM((columns // n_shifts, reals), jnp.bfloat16)] * n_shifts,
        in_specs=[VMEM] * (1 + len(pieces)),
        out_specs=[VMEM] * n_shifts,
        scratch_shapes=[pltpu.VMEM((sites, columns), jnp.bfloat16)],
        compiler_params=vmem(noise.shape, (sites, 2 * columns)),
        cost_estimate=cost(2 * sites * columns * reals, noise, *pieces),
        name=f"project_{n_shifts}",
    )(noise, *pieces)


def stage_kernel(from_ref, to_ref, sems):
    parts = sems.shape[0]
    rows = from_ref.shape[0] // parts
    copies = []
    for part in range(parts):
        span = slice(part * rows, (part + 1) * rows)
        copies.append(
            pltpu.make_async_copy(from_ref.at[span, :], to_ref.at[span, :], sems.at[part])
        )
        copies[-1].start()
    for copy in copies:
        copy.wait()


def stage(array):
    return pl.pallas_call(
        stage_kernel,
        out_shape=jax.ShapeDtypeStruct(array.shape, array.dtype),
        in_specs=[pl.BlockSpec(memory_space=pltpu.HBM)],
        out_specs=VMEM,
        scratch_shapes=[pltpu.SemaphoreType.DMA((4,))],
        compiler_params=vmem(array.shape),
        cost_estimate=cost(0, array),
        name="stage",
    )(array)


def source_of(shift):
    site_count = lax.axis_size("site")
    return lax.rem(lax.axis_index("site") + (site_count - shift), site_count)


def alive_coef(shift, ranks_ref, coef):
    rank = ranks_ref[lax.axis_index("site"), source_of(shift)]
    row = lax.broadcasted_iota(jnp.int32, coef.shape, 0)
    alive = row < rank * (coef.shape[0] // CAP)
    return jnp.where(alive, coef.astype(jnp.float32), 0.0).astype(coef.dtype)


def accumulate_kernel(shifts, places, rows, ranks_ref, noise_ref, *refs):
    pieces, coefs = refs[: len(places)], refs[len(places) : len(places) + len(shifts)]
    u_ref, sum_ref, whole = refs[-3:]
    stack_pieces(places, rows, pieces, whole)
    per_source = whole.shape[1] - u_ref.shape[1]
    u_ref[...] = whole[:, per_source:]
    own = project_columns(whole[:, :per_source], noise_ref)
    total = jnp.zeros(sum_ref.shape, jnp.float32)
    for shift, coef in zip((0,) + shifts, [own] + [coef_ref[...] for coef_ref in coefs]):
        start = pl.multiple_of(source_of(shift) * per_source, per_source)
        total += jnp.dot(
            u_ref[:, pl.ds(start, per_source)],
            alive_coef(shift, ranks_ref, coef),
            preferred_element_type=jnp.float32,
        )
    sum_ref[...] = total


def accumulate(shifts, ranks, noise, gathered, coefs):
    places, pieces = zip(*gathered)
    sites, reals = noise.shape
    rows, columns = sites // lax.axis_size("real"), pieces[0].shape[1]
    per_source = coefs[0].shape[0]
    return pl.pallas_call(
        functools.partial(accumulate_kernel, shifts, places, rows),
        out_shape=[
            jax.ShapeDtypeStruct((sites, columns - per_source), jnp.bfloat16),
            jax.ShapeDtypeStruct((sites, reals), jnp.float32),
        ],
        in_specs=[SMEM] + [VMEM] * (1 + len(pieces) + len(coefs)),
        out_specs=[VMEM] * 2,
        scratch_shapes=[pltpu.VMEM((sites, columns), jnp.bfloat16)],
        compiler_params=vmem((sites, 3 * reals), (sites, 2 * columns)),
        cost_estimate=cost(6 * sites * per_source * reals, noise, *pieces, *coefs),
        name="accumulate",
    )(ranks, noise, *pieces, *coefs)


def finish_kernel(shifts, ranks_ref, u_ref, sum_ref, skew_ref, tail_ref, *refs):
    coefs = refs[: len(shifts)]
    out_ref, slots, sems = refs[len(shifts) :]
    block = slots.shape[1]
    alive = [alive_coef(shift, ranks_ref, coef[...]) for shift, coef in zip(shifts, coefs)]
    copies = []
    for step in range(out_ref.shape[0] // block):
        rows = slice(step * block, (step + 1) * block)
        gaussian = sum_ref[rows, :]
        for shift, coef in zip(shifts, alive):
            columns = coef.shape[0]
            start = pl.multiple_of(source_of(shift) * columns, columns)
            gaussian += jnp.dot(
                u_ref[rows, pl.ds(start, columns)], coef, preferred_element_type=jnp.float32
            )
        skew, tail = skew_ref[rows, :], tail_ref[rows, :]
        grown = jnp.exp2((skew * LOG2E) * gaussian) + 1.0
        grown = grown * jnp.tanh((0.5 * skew) * gaussian) * (1.0 / skew)
        slots[step] = grown * jnp.exp2((0.5 * LOG2E * tail) * (gaussian * gaussian))
        copy = pltpu.make_async_copy(slots.at[step], out_ref.at[rows, :], sems.at[step])
        copy.start()
        copies.append(copy)
    for copy in copies:
        copy.wait()


def finish(shifts, ranks, u_whole, total, skew, tail, coefs):
    rows, columns = u_whole.shape
    per_source, reals = coefs[0].shape
    block = min(rows, 128)
    return pl.pallas_call(
        functools.partial(finish_kernel, shifts),
        out_shape=jax.ShapeDtypeStruct((rows, reals), jnp.float32),
        in_specs=[SMEM] + [VMEM] * (4 + len(coefs)),
        out_specs=pl.BlockSpec(memory_space=pl.ANY),
        scratch_shapes=[
            pltpu.VMEM((rows // block, block, reals), jnp.float32),
            pltpu.SemaphoreType.DMA((rows // block,)),
        ],
        compiler_params=vmem((rows, 4 * reals), u_whole.shape),
        cost_estimate=cost(2 * rows * len(coefs) * per_source * reals, u_whole, total, *coefs),
        name="finish",
    )(ranks, u_whole, total, skew, tail, *coefs)


def after(value, *before):
    return lax.optimization_barrier((value, before))[0]


def swap(array, distance):
    count = lax.axis_size("real")
    return lax.ppermute(array, "real", [(k, k ^ distance) for k in range(count)])


def with_other_core(pieces):
    both = dict(pieces)
    for (distance, row), piece in pieces.items():
        if (distance ^ 1, row) not in pieces:
            both[distance ^ 1, row] = swap(piece, 1)
    return both


def from_chips(own, end=None):
    pieces = {(0, 0): own}
    for distance in range(2, end or lax.axis_size("real"), 2):
        pieces[distance, 0] = swap(own, distance)
    return pieces


def direct_rest(chunk):
    pieces = with_other_core(from_chips(chunk))
    del pieces[0, 0]
    return pieces


def from_other_core(pieces):
    return {place: array for place, array in with_other_core(pieces).items() if place not in pieces}


def at_once(present, gather, *args):
    shapes, tree = [], []

    def flat(*args):
        leaves, structure = jax.tree.flatten(gather(*args))
        tree[:] = [structure]
        return leaves

    shapes = jax.eval_shape(flat, *args)
    nothing = lambda *_: [jnp.zeros(leaf.shape, leaf.dtype) for leaf in shapes]
    return jax.tree.unflatten(tree[0], lax.cond(present, flat, nothing, *args))


def along_site(coef, shift):
    count = lax.axis_size("site")
    return lax.ppermute(coef, "site", [(k, (k + shift) % count) for k in range(count)])


def per_device(noise, v_factors, u_factors, ranks, skew_g, tail_h):
    site_count = lax.axis_size("site")
    real_count = lax.axis_size("real")
    source = lax.axis_index("site")
    rows, columns = v_factors.shape[1:]
    per_dest = columns // site_count
    middle = site_count // 2
    others = sorted(range(1, site_count), key=lambda shift: (abs(shift - middle), shift))
    first, rest = others[0], tuple(others[1:])

    def columns_for(shift):
        start = lax.rem(source + shift, site_count) * per_dest
        return lax.dynamic_slice(v_factors[0], (0, start), (rows, per_dest))

    v_first = columns_for(first)
    v_rest = jnp.concatenate([columns_for(shift) for shift in rest], axis=1)
    own_and_u = jnp.concatenate([columns_for(0), u_factors[0]], axis=1)
    v_first = from_chips(v_first)
    last = max(v_first)
    waiting = (v_first[last], stage(noise), v_rest, own_and_u)
    v_first[last], noise_here, v_rest, own_and_u = lax.optimization_barrier(waiting)
    present = ranks[0, 0] > 0
    noise_here, present = lax.optimization_barrier((noise_here, present))
    opposite = max(v_first)
    u_opposite = swap(after(own_and_u, v_first), opposite[0])
    [far] = project(1, noise_here, with_other_core(v_first).items())

    u_swapped = swap(after(own_and_u, far), 1)
    v_rest = after(v_rest, far, u_opposite, u_swapped)
    v_pieces = {(0, 0): v_rest, **at_once(present, direct_rest, v_rest)}
    u_pieces = {**from_chips(after(own_and_u, v_pieces), opposite[0]), opposite: u_opposite}
    u_pieces[1, 0] = u_swapped
    others = project(len(rest), noise_here, v_pieces.items())
    far = along_site(far, first)
    others = [others[0], *after(others[1:], far)]
    u_pieces.update(at_once(present, from_other_core, u_pieces))
    others = [along_site(coef, shift) for coef, shift in zip(others, rest)]
    u_whole, total = accumulate((first,), ranks, noise, u_pieces.items(), [far])
    return finish(rest, ranks, u_whole, total, skew_g[:, None], tail_h[:, None], others)


def solution(mesh):
    placed = (
        P("site", "real"),
        P("site", "real", None),
        P("site", "real", None),
        P(),
        P("site"),
        P("site"),
    )
    return jax.shard_map(
        per_device, mesh=mesh, in_specs=placed, out_specs=P("site", "real"), check_vma=False
    )
```

```python
import functools
import math

import jax
import jax.numpy as jnp
from jax import lax
from jax.experimental import pallas as pl
from jax.experimental.pallas import tpu as pltpu
from jax.sharding import PartitionSpec as P

CAP = 2
LOG2E = 1.4426950408889634
VMEM = pl.BlockSpec(memory_space=pltpu.VMEM)
SMEM = pl.BlockSpec(memory_space=pltpu.SMEM)


def vmem(*shapes):
    held = sum(4 * math.prod(shape) for shape in shapes)
    return pltpu.CompilerParams(vmem_limit_bytes=held + 6 * 2**20)


def cost(flops, *arrays):
    touched = sum(array.size * array.dtype.itemsize for array in arrays)
    return pl.CostEstimate(flops=flops, bytes_accessed=2 * touched, transcendentals=0)


def stack_pieces(places, rows, pieces, whole):
    me = lax.axis_index("real")
    for (distance, row), piece in zip(places, pieces):
        height = piece.shape[0]
        start = pl.multiple_of((me ^ distance) * rows + row, height)
        whole[pl.ds(start, height), :] = piece[...]


def project_columns(v_columns, noise_ref):
    projected = lax.dot_general(
        v_columns, noise_ref[...], (((0,), (0,)), ((), ())), preferred_element_type=jnp.float32
    )
    return projected.astype(jnp.bfloat16)


def project_kernel(places, rows, noise_ref, *refs):
    pieces, outs, whole = refs[: len(places)], refs[len(places) : -1], refs[-1]
    stack_pieces(places, rows, pieces, whole)
    for place, out_ref in enumerate(outs):
        columns = out_ref.shape[0]
        out_ref[...] = project_columns(
            whole[:, place * columns : (place + 1) * columns], noise_ref
        )


def project(n_shifts, noise, gathered):
    sites, reals = noise.shape
    places, pieces = zip(*gathered)
    rows, columns = pieces[0].shape
    return pl.pallas_call(
        functools.partial(project_kernel, places, rows),
        out_shape=[jax.ShapeDtypeStruct((columns // n_shifts, reals), jnp.bfloat16)] * n_shifts,
        in_specs=[VMEM] * (1 + len(pieces)),
        out_specs=[VMEM] * n_shifts,
        scratch_shapes=[pltpu.VMEM((sites, columns), jnp.bfloat16)],
        compiler_params=vmem(noise.shape, (sites, 2 * columns)),
        cost_estimate=cost(2 * sites * columns * reals, noise, *pieces),
        name=f"project_{n_shifts}",
    )(noise, *pieces)


def stage_kernel(from_ref, to_ref, sems):
    parts = sems.shape[0]
    rows = from_ref.shape[0] // parts
    copies = []
    for part in range(parts):
        span = slice(part * rows, (part + 1) * rows)
        copies.append(
            pltpu.make_async_copy(from_ref.at[span, :], to_ref.at[span, :], sems.at[part])
        )
        copies[-1].start()
    for copy in copies:
        copy.wait()


def stage(array):
    return pl.pallas_call(
        stage_kernel,
        out_shape=jax.ShapeDtypeStruct(array.shape, array.dtype),
        in_specs=[pl.BlockSpec(memory_space=pltpu.HBM)],
        out_specs=VMEM,
        scratch_shapes=[pltpu.SemaphoreType.DMA((4,))],
        compiler_params=vmem(array.shape),
        cost_estimate=cost(0, array),
        name="stage",
    )(array)


def source_of(shift):
    site_count = lax.axis_size("site")
    return lax.rem(lax.axis_index("site") + (site_count - shift), site_count)


def alive_coef(shift, ranks_ref, coef):
    rank = ranks_ref[lax.axis_index("site"), source_of(shift)]
    row = lax.broadcasted_iota(jnp.int32, coef.shape, 0)
    alive = row < rank * (coef.shape[0] // CAP)
    return jnp.where(alive, coef.astype(jnp.float32), 0.0).astype(coef.dtype)


def accumulate_kernel(shifts, places, rows, ranks_ref, noise_ref, *refs):
    pieces, coefs = refs[: len(places)], refs[len(places) : len(places) + len(shifts)]
    u_ref, sum_ref, whole = refs[-3:]
    stack_pieces(places, rows, pieces, whole)
    per_source = whole.shape[1] - u_ref.shape[1]
    u_ref[...] = whole[:, per_source:]
    own = project_columns(whole[:, :per_source], noise_ref)
    total = jnp.zeros(sum_ref.shape, jnp.float32)
    for shift, coef in zip((0,) + shifts, [own] + [coef_ref[...] for coef_ref in coefs]):
        start = pl.multiple_of(source_of(shift) * per_source, per_source)
        total += jnp.dot(
            u_ref[:, pl.ds(start, per_source)],
            alive_coef(shift, ranks_ref, coef),
            preferred_element_type=jnp.float32,
        )
    sum_ref[...] = total


def accumulate(shifts, ranks, noise, gathered, coefs):
    places, pieces = zip(*gathered)
    sites, reals = noise.shape
    rows, columns = sites // lax.axis_size("real"), pieces[0].shape[1]
    per_source = coefs[0].shape[0]
    return pl.pallas_call(
        functools.partial(accumulate_kernel, shifts, places, rows),
        out_shape=[
            jax.ShapeDtypeStruct((sites, columns - per_source), jnp.bfloat16),
            jax.ShapeDtypeStruct((sites, reals), jnp.float32),
        ],
        in_specs=[SMEM] + [VMEM] * (1 + len(pieces) + len(coefs)),
        out_specs=[VMEM] * 2,
        scratch_shapes=[pltpu.VMEM((sites, columns), jnp.bfloat16)],
        compiler_params=vmem((sites, 3 * reals), (sites, 2 * columns)),
        cost_estimate=cost(6 * sites * per_source * reals, noise, *pieces, *coefs),
        name="accumulate",
    )(ranks, noise, *pieces, *coefs)


def as_rows(ref, rows):
    values = ref[:, rows]
    return jnp.transpose(jnp.broadcast_to(values, (values.shape[1], values.shape[1])))


def finish_kernel(shifts, ranks_ref, u_ref, sum_ref, skew_ref, tail_ref, *refs):
    coefs = refs[: len(shifts)]
    out_ref, slots, sems = refs[len(shifts) :]
    block = slots.shape[1]
    alive = [alive_coef(shift, ranks_ref, coef[...]) for shift, coef in zip(shifts, coefs)]
    copies = []
    for step in range(out_ref.shape[0] // block):
        rows = slice(step * block, (step + 1) * block)
        gaussian = sum_ref[rows, :]
        for shift, coef in zip(shifts, alive):
            columns = coef.shape[0]
            start = pl.multiple_of(source_of(shift) * columns, columns)
            gaussian += jnp.dot(
                u_ref[rows, pl.ds(start, columns)], coef, preferred_element_type=jnp.float32
            )
        skew, tail = as_rows(skew_ref, rows), as_rows(tail_ref, rows)
        growth, turn, scale = LOG2E * skew, 0.5 * skew, 1.0 / skew
        spread = (0.5 * LOG2E) * tail
        lanes = skew.shape[1]
        for start in range(0, gaussian.shape[1], lanes):
            at = gaussian[:, start : start + lanes]
            grown = (jnp.exp2(growth * at) + 1.0) * jnp.tanh(turn * at) * scale
            slots[step, :, start : start + lanes] = grown * jnp.exp2(spread * (at * at))
        copy = pltpu.make_async_copy(slots.at[step], out_ref.at[rows, :], sems.at[step])
        copy.start()
        copies.append(copy)
    for copy in copies:
        copy.wait()


def finish(shifts, ranks, u_whole, total, skew, tail, coefs):
    rows, columns = u_whole.shape
    per_source, reals = coefs[0].shape
    block = min(rows, 128)
    return pl.pallas_call(
        functools.partial(finish_kernel, shifts),
        out_shape=jax.ShapeDtypeStruct((rows, reals), jnp.float32),
        in_specs=[SMEM] + [VMEM] * (4 + len(coefs)),
        out_specs=pl.BlockSpec(memory_space=pl.ANY),
        scratch_shapes=[
            pltpu.VMEM((rows // block, block, reals), jnp.float32),
            pltpu.SemaphoreType.DMA((rows // block,)),
        ],
        compiler_params=vmem((rows, 4 * reals), u_whole.shape),
        cost_estimate=cost(2 * rows * len(coefs) * per_source * reals, u_whole, total, *coefs),
        name="finish",
    )(ranks, u_whole, total, skew, tail, *coefs)


def after(value, *before):
    return lax.optimization_barrier((value, before))[0]


def swap(array, distance):
    count = lax.axis_size("real")
    return lax.ppermute(array, "real", [(k, k ^ distance) for k in range(count)])


def with_other_core(pieces):
    both = dict(pieces)
    for (distance, row), piece in pieces.items():
        if (distance ^ 1, row) not in pieces:
            both[distance ^ 1, row] = swap(piece, 1)
    return both


def from_chips(own):
    pieces = {(0, 0): own}
    for distance in range(2, lax.axis_size("real"), 2):
        pieces[distance, 0] = swap(own, distance)
    return pieces


def direct_rest(chunk):
    pieces = with_other_core(from_chips(chunk))
    del pieces[0, 0]
    return pieces


def from_other_core(pieces):
    return {place: array for place, array in with_other_core(pieces).items() if place not in pieces}


def at_once(present, gather, *args):
    shapes, tree = [], []

    def flat(*args):
        leaves, structure = jax.tree.flatten(gather(*args))
        tree[:] = [structure]
        return leaves

    shapes = jax.eval_shape(flat, *args)
    nothing = lambda *_: [jnp.zeros(leaf.shape, leaf.dtype) for leaf in shapes]
    return jax.tree.unflatten(tree[0], lax.cond(present, flat, nothing, *args))


def along_site(coef, shift):
    count = lax.axis_size("site")
    return lax.ppermute(coef, "site", [(k, (k + shift) % count) for k in range(count)])


def per_device(noise, v_factors, u_factors, ranks, skew_g, tail_h):
    site_count = lax.axis_size("site")
    real_count = lax.axis_size("real")
    source = lax.axis_index("site")
    rows, columns = v_factors.shape[1:]
    per_dest = columns // site_count
    middle = site_count // 2
    others = sorted(range(1, site_count), key=lambda shift: (abs(shift - middle), shift))
    first, rest = others[0], tuple(others[1:])

    def columns_for(shift):
        start = lax.rem(source + shift, site_count) * per_dest
        return lax.dynamic_slice(v_factors[0], (0, start), (rows, per_dest))

    v_first = columns_for(first)
    v_rest = jnp.concatenate([columns_for(shift) for shift in rest], axis=1)
    own_and_u = jnp.concatenate([columns_for(0), u_factors[0]], axis=1)
    v_first = from_chips(v_first)
    last = max(v_first)
    waiting = (v_first[last], stage(noise), v_rest, own_and_u)
    v_first[last], noise_here, v_rest, own_and_u = lax.optimization_barrier(waiting)
    present = ranks[0, 0] > 0
    noise_here, present = lax.optimization_barrier((noise_here, present))
    [far] = project(1, noise_here, with_other_core(v_first).items())

    u_swapped = swap(after(own_and_u, far), 1)
    v_rest = after(v_rest, far, u_swapped)
    v_pieces = {(0, 0): v_rest, **at_once(present, direct_rest, v_rest)}
    u_pieces = from_chips(after(own_and_u, v_pieces))
    others = project(len(rest), noise_here, v_pieces.items())
    far = along_site(far, first)
    others = [others[0], *after(others[1:], far)]
    u_pieces = {**u_pieces, (1, 0): u_swapped}
    u_pieces.update(at_once(present, from_other_core, u_pieces))
    others = [along_site(coef, shift) for coef, shift in zip(others, rest)]
    u_whole, total = accumulate((first,), ranks, noise, u_pieces.items(), [far])
    return finish(rest, ranks, u_whole, total, skew_g[None], tail_h[None], others)


def solution(mesh):
    placed = (
        P("site", "real"),
        P("site", "real", None),
        P("site", "real", None),
        P(),
        P("site"),
        P("site"),
    )
    return jax.shard_map(
        per_device, mesh=mesh, in_specs=placed, out_specs=P("site", "real"), check_vma=False
    )
```

```python
import functools
import math

import jax
import jax.numpy as jnp
from jax import lax
from jax.experimental import pallas as pl
from jax.experimental.pallas import tpu as pltpu
from jax.sharding import PartitionSpec as P

CAP = 2
LOG2E = 1.4426950408889634
VMEM = pl.BlockSpec(memory_space=pltpu.VMEM)
SMEM = pl.BlockSpec(memory_space=pltpu.SMEM)


def vmem(*shapes):
    held = sum(4 * math.prod(shape) for shape in shapes)
    return pltpu.CompilerParams(vmem_limit_bytes=held + 6 * 2**20)


def cost(flops, *arrays):
    touched = sum(array.size * array.dtype.itemsize for array in arrays)
    return pl.CostEstimate(flops=flops, bytes_accessed=2 * touched, transcendentals=0)


def stack_pieces(places, rows, pieces, whole):
    me = lax.axis_index("real")
    for (distance, row), piece in zip(places, pieces):
        height = piece.shape[0]
        start = pl.multiple_of((me ^ distance) * rows + row, height)
        whole[pl.ds(start, height), :] = piece[...]


def project_columns(v_columns, noise_ref):
    projected = lax.dot_general(
        v_columns, noise_ref[...], (((0,), (0,)), ((), ())), preferred_element_type=jnp.float32
    )
    return projected.astype(jnp.bfloat16)


def project_kernel(places, rows, noise_ref, *refs):
    pieces, outs, whole = refs[: len(places)], refs[len(places) : -1], refs[-1]
    stack_pieces(places, rows, pieces, whole)
    for place, out_ref in enumerate(outs):
        columns = out_ref.shape[0]
        out_ref[...] = project_columns(
            whole[:, place * columns : (place + 1) * columns], noise_ref
        )


def project(n_shifts, noise, gathered):
    sites, reals = noise.shape
    places, pieces = zip(*gathered)
    rows, columns = pieces[0].shape
    return pl.pallas_call(
        functools.partial(project_kernel, places, rows),
        out_shape=[jax.ShapeDtypeStruct((columns // n_shifts, reals), jnp.bfloat16)] * n_shifts,
        in_specs=[VMEM] * (1 + len(pieces)),
        out_specs=[VMEM] * n_shifts,
        scratch_shapes=[pltpu.VMEM((sites, columns), jnp.bfloat16)],
        compiler_params=vmem(noise.shape, (sites, 2 * columns)),
        cost_estimate=cost(2 * sites * columns * reals, noise, *pieces),
        name=f"project_{n_shifts}",
    )(noise, *pieces)


def stage_kernel(from_ref, to_ref, sems):
    parts = sems.shape[0]
    rows = from_ref.shape[0] // parts
    copies = []
    for part in range(parts):
        span = slice(part * rows, (part + 1) * rows)
        copies.append(
            pltpu.make_async_copy(from_ref.at[span, :], to_ref.at[span, :], sems.at[part])
        )
        copies[-1].start()
    for copy in copies:
        copy.wait()


def stage(array):
    return pl.pallas_call(
        stage_kernel,
        out_shape=jax.ShapeDtypeStruct(array.shape, array.dtype),
        in_specs=[pl.BlockSpec(memory_space=pltpu.HBM)],
        out_specs=VMEM,
        scratch_shapes=[pltpu.SemaphoreType.DMA((4,))],
        compiler_params=vmem(array.shape),
        cost_estimate=cost(0, array),
        name="stage",
    )(array)


def source_of(shift):
    site_count = lax.axis_size("site")
    return lax.rem(lax.axis_index("site") + (site_count - shift), site_count)


def alive_coef(shift, ranks_ref, coef):
    rank = ranks_ref[lax.axis_index("site"), source_of(shift)]
    row = lax.broadcasted_iota(jnp.int32, coef.shape, 0)
    alive = row < rank * (coef.shape[0] // CAP)
    return jnp.where(alive, coef.astype(jnp.float32), 0.0).astype(coef.dtype)


def accumulate_kernel(shifts, places, rows, ranks_ref, noise_ref, *refs):
    pieces, coefs = refs[: len(places)], refs[len(places) : len(places) + len(shifts)]
    u_ref, sum_ref, whole = refs[-3:]
    stack_pieces(places, rows, pieces, whole)
    per_source = whole.shape[1] - u_ref.shape[1]
    u_ref[...] = whole[:, per_source:]
    own = project_columns(whole[:, :per_source], noise_ref)
    total = jnp.zeros(sum_ref.shape, jnp.float32)
    for shift, coef in zip((0,) + shifts, [own] + [coef_ref[...] for coef_ref in coefs]):
        start = pl.multiple_of(source_of(shift) * per_source, per_source)
        total += jnp.dot(
            u_ref[:, pl.ds(start, per_source)],
            alive_coef(shift, ranks_ref, coef),
            preferred_element_type=jnp.float32,
        )
    sum_ref[...] = total


def accumulate(shifts, ranks, noise, gathered, coefs):
    places, pieces = zip(*gathered)
    sites, reals = noise.shape
    rows, columns = sites // lax.axis_size("real"), pieces[0].shape[1]
    per_source = coefs[0].shape[0]
    return pl.pallas_call(
        functools.partial(accumulate_kernel, shifts, places, rows),
        out_shape=[
            jax.ShapeDtypeStruct((sites, columns - per_source), jnp.bfloat16),
            jax.ShapeDtypeStruct((sites, reals), jnp.float32),
        ],
        in_specs=[SMEM] + [VMEM] * (1 + len(pieces) + len(coefs)),
        out_specs=[VMEM] * 2,
        scratch_shapes=[pltpu.VMEM((sites, columns), jnp.bfloat16)],
        compiler_params=vmem((sites, 3 * reals), (sites, 2 * columns)),
        cost_estimate=cost(6 * sites * per_source * reals, noise, *pieces, *coefs),
        name="accumulate",
    )(ranks, noise, *pieces, *coefs)


def as_rows(ref, rows):
    values = ref[:, rows]
    return jnp.transpose(jnp.broadcast_to(values, (values.shape[1], values.shape[1])))


def finish_kernel(shifts, ranks_ref, u_ref, sum_ref, skew_ref, tail_ref, *refs):
    coefs = refs[: len(shifts)]
    out_ref, slots, sems = refs[len(shifts) :]
    block = slots.shape[1]
    alive = [alive_coef(shift, ranks_ref, coef[...]) for shift, coef in zip(shifts, coefs)]
    copies = []
    for step in range(out_ref.shape[0] // block):
        rows = slice(step * block, (step + 1) * block)
        gaussian = sum_ref[rows, :]
        for shift, coef in zip(shifts, alive):
            columns = coef.shape[0]
            start = pl.multiple_of(source_of(shift) * columns, columns)
            gaussian += jnp.dot(
                u_ref[rows, pl.ds(start, columns)], coef, preferred_element_type=jnp.float32
            )
        skew, tail = as_rows(skew_ref, rows), as_rows(tail_ref, rows)
        growth, turn, scale = LOG2E * skew, 0.5 * skew, 1.0 / skew
        spread = (0.5 * LOG2E) * tail
        lanes = skew.shape[1]
        for start in range(0, gaussian.shape[1], lanes):
            at = gaussian[:, start : start + lanes]
            grown = (jnp.exp2(growth * at) + 1.0) * jnp.tanh(turn * at) * scale
            slots[step, :, start : start + lanes] = grown * jnp.exp2(spread * (at * at))
        copy = pltpu.make_async_copy(slots.at[step], out_ref.at[rows, :], sems.at[step])
        copy.start()
        copies.append(copy)
    for copy in copies:
        copy.wait()


def finish(shifts, ranks, u_whole, total, skew, tail, coefs):
    rows, columns = u_whole.shape
    per_source, reals = coefs[0].shape
    block = min(rows, 128)
    return pl.pallas_call(
        functools.partial(finish_kernel, shifts),
        out_shape=jax.ShapeDtypeStruct((rows, reals), jnp.float32),
        in_specs=[SMEM] + [VMEM] * (4 + len(coefs)),
        out_specs=pl.BlockSpec(memory_space=pl.ANY),
        scratch_shapes=[
            pltpu.VMEM((rows // block, block, reals), jnp.float32),
            pltpu.SemaphoreType.DMA((rows // block,)),
        ],
        compiler_params=vmem((rows, 4 * reals), u_whole.shape),
        cost_estimate=cost(2 * rows * len(coefs) * per_source * reals, u_whole, total, *coefs),
        name="finish",
    )(ranks, u_whole, total, skew, tail, *coefs)


def after(value, *before):
    return lax.optimization_barrier((value, before))[0]


def swap(array, distance):
    count = lax.axis_size("real")
    return lax.ppermute(array, "real", [(k, k ^ distance) for k in range(count)])


def with_other_core(pieces):
    both = dict(pieces)
    for (distance, row), piece in pieces.items():
        if (distance ^ 1, row) not in pieces:
            both[distance ^ 1, row] = swap(piece, 1)
    return both


def from_chips(own):
    pieces = {(0, 0): own}
    for distance in range(2, lax.axis_size("real"), 2):
        pieces[distance, 0] = swap(own, distance)
    return pieces


def from_other_core(pieces):
    return {place: array for place, array in with_other_core(pieces).items() if place not in pieces}


def at_once(present, gather, pieces):
    places, arrays, new = list(pieces), list(pieces.values()), []

    def added(*arrays):
        more = gather(dict(zip(places, arrays)))
        new[:] = [place for place in more if place not in pieces]
        return [more[place] for place in new]

    count = len(jax.eval_shape(added, *arrays))
    results = lax.cond(present, added, lambda *same: [same[0]] * count, *arrays)
    return dict(zip(new, results))


def along_site(coef, shift):
    count = lax.axis_size("site")
    return lax.ppermute(coef, "site", [(k, (k + shift) % count) for k in range(count)])


def per_device(noise, v_factors, u_factors, ranks, skew_g, tail_h):
    site_count = lax.axis_size("site")
    real_count = lax.axis_size("real")
    source = lax.axis_index("site")
    rows, columns = v_factors.shape[1:]
    per_dest = columns // site_count
    middle = site_count // 2
    others = sorted(range(1, site_count), key=lambda shift: (abs(shift - middle), shift))
    first, rest = others[0], tuple(others[1:])

    def columns_for(shift):
        start = lax.rem(source + shift, site_count) * per_dest
        return lax.dynamic_slice(v_factors[0], (0, start), (rows, per_dest))

    v_first = columns_for(first)
    v_rest = jnp.concatenate([columns_for(shift) for shift in rest], axis=1)
    own_and_u = jnp.concatenate([columns_for(0), u_factors[0]], axis=1)
    v_first = from_chips(v_first)
    last = max(v_first)
    waiting = (v_first[last], stage(noise), v_rest, own_and_u)
    v_first[last], noise_here, v_rest, own_and_u = lax.optimization_barrier(waiting)
    present = ranks[0, 0] > 0
    noise_here, present = lax.optimization_barrier((noise_here, present))
    [far] = project(1, noise_here, with_other_core(v_first).items())

    u_swapped = swap(after(own_and_u, far), 1)
    v_rest = after(v_rest, far, u_swapped)
    v_pieces = {(0, 0): v_rest}
    v_pieces.update(at_once(present, lambda own: with_other_core(from_chips(own[0, 0])), v_pieces))
    u_pieces = from_chips(after(own_and_u, v_pieces))
    others = project(len(rest), noise_here, v_pieces.items())
    far = along_site(far, first)
    others = [others[0], *after(others[1:], far)]
    u_pieces = {**u_pieces, (1, 0): u_swapped}
    u_pieces.update(at_once(present, from_other_core, u_pieces))
    others = [along_site(coef, shift) for coef, shift in zip(others, rest)]
    u_whole, total = accumulate((first,), ranks, noise, u_pieces.items(), [far])
    return finish(rest, ranks, u_whole, total, skew_g[None], tail_h[None], others)


def solution(mesh):
    placed = (
        P("site", "real"),
        P("site", "real", None),
        P("site", "real", None),
        P(),
        P("site"),
        P("site"),
    )
    return jax.shard_map(
        per_device, mesh=mesh, in_specs=placed, out_specs=P("site", "real"), check_vma=False
    )
```

```python
import functools
import math

import jax
import jax.numpy as jnp
from jax import lax
from jax.experimental import pallas as pl
from jax.experimental.pallas import tpu as pltpu
from jax.sharding import PartitionSpec as P

CAP = 2
LOG2E = 1.4426950408889634
VMEM = pl.BlockSpec(memory_space=pltpu.VMEM)
SMEM = pl.BlockSpec(memory_space=pltpu.SMEM)


def vmem(*shapes):
    held = sum(4 * math.prod(shape) for shape in shapes)
    return pltpu.CompilerParams(vmem_limit_bytes=held + 6 * 2**20)


def cost(flops, *arrays):
    touched = sum(array.size * array.dtype.itemsize for array in arrays)
    return pl.CostEstimate(flops=flops, bytes_accessed=2 * touched, transcendentals=0)


def stack_pieces(mine, others, whole):
    core = lax.rem(lax.axis_index("real"), 2)
    chips, rows, _ = mine.shape
    for chip in range(chips):
        for place, pieces in ((core, mine), (1 - core, others)):
            start = pl.multiple_of((2 * chip + place) * rows, rows)
            whole[pl.ds(start, rows), :] = pieces[chip]


def project_columns(v_columns, noise_ref):
    projected = lax.dot_general(
        v_columns, noise_ref[...], (((0,), (0,)), ((), ())), preferred_element_type=jnp.float32
    )
    return projected.astype(jnp.bfloat16)


def project_kernel(noise_ref, mine, others, *refs):
    outs, whole = refs[:-1], refs[-1]
    stack_pieces(mine, others, whole)
    for place, out_ref in enumerate(outs):
        columns = out_ref.shape[0]
        out_ref[...] = project_columns(
            whole[:, place * columns : (place + 1) * columns], noise_ref
        )


def project(n_shifts, noise, mine, others):
    sites, reals = noise.shape
    columns = mine.shape[2]
    return pl.pallas_call(
        project_kernel,
        out_shape=[jax.ShapeDtypeStruct((columns // n_shifts, reals), jnp.bfloat16)] * n_shifts,
        in_specs=[VMEM] * 3,
        out_specs=[VMEM] * n_shifts,
        scratch_shapes=[pltpu.VMEM((sites, columns), jnp.bfloat16)],
        compiler_params=vmem(noise.shape, (sites, 2 * columns)),
        cost_estimate=cost(2 * sites * columns * reals, noise, mine, others),
        name=f"project_{n_shifts}",
    )(noise, mine, others)


def stage_kernel(from_ref, to_ref, sems):
    parts = sems.shape[0]
    rows = from_ref.shape[0] // parts
    copies = []
    for part in range(parts):
        span = slice(part * rows, (part + 1) * rows)
        copies.append(
            pltpu.make_async_copy(from_ref.at[span, :], to_ref.at[span, :], sems.at[part])
        )
        copies[-1].start()
    for copy in copies:
        copy.wait()


def stage(array):
    return pl.pallas_call(
        stage_kernel,
        out_shape=jax.ShapeDtypeStruct(array.shape, array.dtype),
        in_specs=[pl.BlockSpec(memory_space=pltpu.HBM)],
        out_specs=VMEM,
        scratch_shapes=[pltpu.SemaphoreType.DMA((4,))],
        compiler_params=vmem(array.shape),
        cost_estimate=cost(0, array),
        name="stage",
    )(array)


def source_of(shift):
    site_count = lax.axis_size("site")
    return lax.rem(lax.axis_index("site") + (site_count - shift), site_count)


def alive_coef(shift, ranks_ref, coef):
    rank = ranks_ref[lax.axis_index("site"), source_of(shift)]
    row = lax.broadcasted_iota(jnp.int32, coef.shape, 0)
    alive = row < rank * (coef.shape[0] // CAP)
    return jnp.where(alive, coef.astype(jnp.float32), 0.0).astype(coef.dtype)


def accumulate_kernel(shifts, ranks_ref, noise_ref, mine, others, *refs):
    coefs = refs[: len(shifts)]
    u_ref, sum_ref, whole = refs[-3:]
    stack_pieces(mine, others, whole)
    per_source = whole.shape[1] - u_ref.shape[1]
    u_ref[...] = whole[:, per_source:]
    own = project_columns(whole[:, :per_source], noise_ref)
    total = jnp.zeros(sum_ref.shape, jnp.float32)
    for shift, coef in zip((0,) + shifts, [own] + [coef_ref[...] for coef_ref in coefs]):
        start = pl.multiple_of(source_of(shift) * per_source, per_source)
        total += jnp.dot(
            u_ref[:, pl.ds(start, per_source)],
            alive_coef(shift, ranks_ref, coef),
            preferred_element_type=jnp.float32,
        )
    sum_ref[...] = total


def accumulate(shifts, ranks, noise, mine, others, coefs):
    sites, reals = noise.shape
    columns = mine.shape[2]
    per_source = coefs[0].shape[0]
    return pl.pallas_call(
        functools.partial(accumulate_kernel, shifts),
        out_shape=[
            jax.ShapeDtypeStruct((sites, columns - per_source), jnp.bfloat16),
            jax.ShapeDtypeStruct((sites, reals), jnp.float32),
        ],
        in_specs=[SMEM] + [VMEM] * (3 + len(coefs)),
        out_specs=[VMEM] * 2,
        scratch_shapes=[pltpu.VMEM((sites, columns), jnp.bfloat16)],
        compiler_params=vmem((sites, 3 * reals), (sites, 2 * columns)),
        cost_estimate=cost(6 * sites * per_source * reals, noise, mine, others, *coefs),
        name="accumulate",
    )(ranks, noise, mine, others, *coefs)


def as_rows(ref, rows):
    values = ref[:, rows]
    return jnp.transpose(jnp.broadcast_to(values, (values.shape[1], values.shape[1])))


def finish_kernel(shifts, ranks_ref, u_ref, sum_ref, skew_ref, tail_ref, *refs):
    coefs = refs[: len(shifts)]
    out_ref, slots, sems = refs[len(shifts) :]
    block = slots.shape[1]
    alive = [alive_coef(shift, ranks_ref, coef[...]) for shift, coef in zip(shifts, coefs)]
    copies = []
    for step in range(out_ref.shape[0] // block):
        rows = slice(step * block, (step + 1) * block)
        gaussian = sum_ref[rows, :]
        for shift, coef in zip(shifts, alive):
            columns = coef.shape[0]
            start = pl.multiple_of(source_of(shift) * columns, columns)
            gaussian += jnp.dot(
                u_ref[rows, pl.ds(start, columns)], coef, preferred_element_type=jnp.float32
            )
        skew, tail = as_rows(skew_ref, rows), as_rows(tail_ref, rows)
        growth, turn, scale = LOG2E * skew, 0.5 * skew, 1.0 / skew
        spread = (0.5 * LOG2E) * tail
        lanes = skew.shape[1]
        for start in range(0, gaussian.shape[1], lanes):
            at = gaussian[:, start : start + lanes]
            grown = (jnp.exp2(growth * at) + 1.0) * jnp.tanh(turn * at) * scale
            slots[step, :, start : start + lanes] = grown * jnp.exp2(spread * (at * at))
        copy = pltpu.make_async_copy(slots.at[step], out_ref.at[rows, :], sems.at[step])
        copy.start()
        copies.append(copy)
    for copy in copies:
        copy.wait()


def finish(shifts, ranks, u_whole, total, skew, tail, coefs):
    rows, columns = u_whole.shape
    per_source, reals = coefs[0].shape
    block = min(rows, 128)
    return pl.pallas_call(
        functools.partial(finish_kernel, shifts),
        out_shape=jax.ShapeDtypeStruct((rows, reals), jnp.float32),
        in_specs=[SMEM] + [VMEM] * (4 + len(coefs)),
        out_specs=pl.BlockSpec(memory_space=pl.ANY),
        scratch_shapes=[
            pltpu.VMEM((rows // block, block, reals), jnp.float32),
            pltpu.SemaphoreType.DMA((rows // block,)),
        ],
        compiler_params=vmem((rows, 4 * reals), u_whole.shape),
        cost_estimate=cost(2 * rows * len(coefs) * per_source * reals, u_whole, total, *coefs),
        name="finish",
    )(ranks, u_whole, total, skew, tail, *coefs)


def after(value, *before):
    return lax.optimization_barrier((value, before))[0]


def repeated(own):
    return jnp.broadcast_to(own, (lax.axis_size("real") // 2, *own.shape))


def from_chips(copies):
    count = lax.axis_size("real")
    cores = [list(range(core, count, 2)) for core in range(2)]
    return lax.all_to_all(copies, "real", 0, 0, axis_index_groups=cores, tiled=True)


def from_other_core(pieces):
    count = lax.axis_size("real")
    return lax.ppermute(pieces, "real", [(k, k ^ 1) for k in range(count)])


def both(copies):
    mine = from_chips(copies)
    return mine, from_other_core(mine)


def at_once(present, gather, array):
    shapes = jax.eval_shape(gather, array)
    same = lambda array: jax.tree.map(lambda _: array, shapes)
    return lax.cond(present, gather, same, array)


def along_site(coef, shift):
    count = lax.axis_size("site")
    return lax.ppermute(coef, "site", [(k, (k + shift) % count) for k in range(count)])


def per_device(noise, v_factors, u_factors, ranks, skew_g, tail_h):
    site_count = lax.axis_size("site")
    real_count = lax.axis_size("real")
    source = lax.axis_index("site")
    rows, columns = v_factors.shape[1:]
    per_dest = columns // site_count
    middle = site_count // 2
    others = sorted(range(1, site_count), key=lambda shift: (abs(shift - middle), shift))
    first, rest = others[0], tuple(others[1:])

    def columns_for(shift):
        start = lax.rem(source + shift, site_count) * per_dest
        return lax.dynamic_slice(v_factors[0], (0, start), (rows, per_dest))

    v_first = from_chips(repeated(columns_for(first)))
    v_rest = repeated(jnp.concatenate([columns_for(shift) for shift in rest], axis=1))
    own_and_u = repeated(jnp.concatenate([columns_for(0), u_factors[0]], axis=1))
    waiting = (v_first, stage(noise), v_rest, own_and_u)
    v_first, noise_here, v_rest, own_and_u = lax.optimization_barrier(waiting)
    present = ranks[0, 0] > 0
    noise_here, present = lax.optimization_barrier((noise_here, present))
    [far] = project(1, noise_here, v_first, from_other_core(v_first))

    v_pieces = at_once(present, both, after(v_rest, far))
    u_mine = from_chips(after(own_and_u, v_pieces))
    others = project(len(rest), noise_here, *v_pieces)
    far = along_site(far, first)
    u_mine = after(u_mine, others[0])
    u_others = at_once(present, from_other_core, u_mine)
    others = [along_site(coef, shift) for coef, shift in zip(others, rest)]
    u_whole, total = accumulate((first,), ranks, noise, u_mine, u_others, [far])
    return finish(rest, ranks, u_whole, total, skew_g[None], tail_h[None], others)


def solution(mesh):
    placed = (
        P("site", "real"),
        P("site", "real", None),
        P("site", "real", None),
        P(),
        P("site"),
        P("site"),
    )
    return jax.shard_map(
        per_device, mesh=mesh, in_specs=placed, out_specs=P("site", "real"), check_vma=False
    )
```

```python
import functools
import math

import jax
import jax.numpy as jnp
from jax import lax
from jax.experimental import pallas as pl
from jax.experimental.pallas import tpu as pltpu
from jax.sharding import PartitionSpec as P

CAP = 2
LOG2E = 1.4426950408889634
VMEM = pl.BlockSpec(memory_space=pltpu.VMEM)
SMEM = pl.BlockSpec(memory_space=pltpu.SMEM)


def vmem(*shapes):
    held = sum(4 * math.prod(shape) for shape in shapes)
    return pltpu.CompilerParams(vmem_limit_bytes=held + 6 * 2**20)


def cost(flops, *arrays):
    touched = sum(array.size * array.dtype.itemsize for array in arrays)
    return pl.CostEstimate(flops=flops, bytes_accessed=2 * touched, transcendentals=0)


def stack_pieces(places, rows, pieces, whole):
    me = lax.axis_index("real")
    for (distance, row), piece in zip(places, pieces):
        height = piece.shape[0]
        start = pl.multiple_of((me ^ distance) * rows + row, height)
        whole[pl.ds(start, height), :] = piece[...]


def project_columns(v_columns, noise_ref):
    projected = lax.dot_general(
        v_columns, noise_ref[...], (((0,), (0,)), ((), ())), preferred_element_type=jnp.float32
    )
    return projected.astype(jnp.bfloat16)


def project_kernel(places, rows, noise_ref, *refs):
    pieces, outs = refs[: len(places)], refs[len(places) : -4]
    whole, results, in_sems, out_sems = refs[-4:]
    me = lax.axis_index("real")
    arriving = []
    for number, ((distance, row), piece) in enumerate(zip(places, pieces)):
        height = piece.shape[0]
        start = pl.multiple_of((me ^ distance) * rows + row, height)
        copy = pltpu.make_async_copy(piece, whole.at[pl.ds(start, height), :], in_sems.at[number])
        copy.start()
        arriving.append(copy)
    for copy in arriving:
        copy.wait()
    leaving = []
    halves = out_sems.shape[0] // len(outs)
    for place, out_ref in enumerate(outs):
        block = out_ref.shape[0] // halves
        for half in range(halves):
            number = place * halves + half
            results[number] = project_columns(
                whole[:, number * block : (number + 1) * block], noise_ref
            )
            span = pl.ds(half * block, block)
            copy = pltpu.make_async_copy(
                results.at[number], out_ref.at[span, :], out_sems.at[number]
            )
            copy.start()
            leaving.append(copy)
    for copy in leaving:
        copy.wait()


def project(n_shifts, noise, gathered):
    sites, reals = noise.shape
    places, pieces = zip(*gathered)
    rows, columns = pieces[0].shape
    halves = 2 if n_shifts == 1 else 1
    count = n_shifts * halves
    anywhere = pl.BlockSpec(memory_space=pl.ANY)
    return pl.pallas_call(
        functools.partial(project_kernel, places, rows),
        out_shape=[jax.ShapeDtypeStruct((columns // n_shifts, reals), jnp.bfloat16)] * n_shifts,
        in_specs=[VMEM] + [anywhere] * len(pieces),
        out_specs=[anywhere] * n_shifts,
        scratch_shapes=[
            pltpu.VMEM((sites, columns), jnp.bfloat16),
            pltpu.VMEM((count, columns // count, reals), jnp.bfloat16),
            pltpu.SemaphoreType.DMA((len(pieces),)),
            pltpu.SemaphoreType.DMA((count,)),
        ],
        compiler_params=vmem(noise.shape, (sites, 2 * columns), (columns, reals)),
        cost_estimate=cost(2 * sites * columns * reals, noise, *pieces),
        name=f"project_{n_shifts}",
    )(noise, *pieces)


def stage_kernel(from_ref, to_ref, sems):
    parts = sems.shape[0]
    rows = from_ref.shape[0] // parts
    copies = []
    for part in range(parts):
        span = slice(part * rows, (part + 1) * rows)
        copies.append(
            pltpu.make_async_copy(from_ref.at[span, :], to_ref.at[span, :], sems.at[part])
        )
        copies[-1].start()
    for copy in copies:
        copy.wait()


def stage(array):
    return pl.pallas_call(
        stage_kernel,
        out_shape=jax.ShapeDtypeStruct(array.shape, array.dtype),
        in_specs=[pl.BlockSpec(memory_space=pltpu.HBM)],
        out_specs=VMEM,
        scratch_shapes=[pltpu.SemaphoreType.DMA((4,))],
        compiler_params=vmem(array.shape),
        cost_estimate=cost(0, array),
        name="stage",
    )(array)


def source_of(shift):
    site_count = lax.axis_size("site")
    return lax.rem(lax.axis_index("site") + (site_count - shift), site_count)


def alive_coef(shift, ranks_ref, coef):
    rank = ranks_ref[lax.axis_index("site"), source_of(shift)]
    row = lax.broadcasted_iota(jnp.int32, coef.shape, 0)
    alive = row < rank * (coef.shape[0] // CAP)
    return jnp.where(alive, coef.astype(jnp.float32), 0.0).astype(coef.dtype)


def as_rows(ref, rows):
    values = ref[:, rows]
    return jnp.transpose(jnp.broadcast_to(values, (values.shape[1], values.shape[1])))


def accumulate_kernel(shifts, places, rows, ranks_ref, noise_ref, skew_ref, tail_ref, *refs):
    pieces, coefs = refs[: len(places)], refs[len(places) : len(places) + len(shifts)]
    u_ref, sum_ref, skew_rows, tail_rows, whole = refs[-5:]
    stack_pieces(places, rows, pieces, whole)
    per_source = whole.shape[1] - u_ref.shape[1]
    u_ref[...] = whole[:, per_source:]
    own = project_columns(whole[:, :per_source], noise_ref)
    total = jnp.zeros(sum_ref.shape, jnp.float32)
    for shift, coef in zip((0,) + shifts, [own] + [coef_ref[...] for coef_ref in coefs]):
        start = pl.multiple_of(source_of(shift) * per_source, per_source)
        total += jnp.dot(
            u_ref[:, pl.ds(start, per_source)],
            alive_coef(shift, ranks_ref, coef),
            preferred_element_type=jnp.float32,
        )
    sum_ref[...] = total
    lanes = skew_rows.shape[1]
    for start in range(0, skew_rows.shape[0], lanes):
        part = slice(start, start + lanes)
        skew_rows[part, :], tail_rows[part, :] = as_rows(skew_ref, part), as_rows(tail_ref, part)


def accumulate(shifts, ranks, noise, skew, tail, gathered, coefs):
    places, pieces = zip(*gathered)
    sites, reals = noise.shape
    rows, columns = sites // lax.axis_size("real"), pieces[0].shape[1]
    per_source = coefs[0].shape[0]
    return pl.pallas_call(
        functools.partial(accumulate_kernel, shifts, places, rows),
        out_shape=[
            jax.ShapeDtypeStruct((sites, columns - per_source), jnp.bfloat16),
            jax.ShapeDtypeStruct((sites, reals), jnp.float32),
            jax.ShapeDtypeStruct((sites, min(sites, 128)), jnp.float32),
            jax.ShapeDtypeStruct((sites, min(sites, 128)), jnp.float32),
        ],
        in_specs=[SMEM] + [VMEM] * (3 + len(pieces) + len(coefs)),
        out_specs=[VMEM] * 4,
        scratch_shapes=[pltpu.VMEM((sites, columns), jnp.bfloat16)],
        compiler_params=vmem((sites, 3 * reals), (sites, 2 * columns)),
        cost_estimate=cost(6 * sites * per_source * reals, noise, *pieces, *coefs),
        name="accumulate",
    )(ranks, noise, skew, tail, *pieces, *coefs)


def finish_kernel(shifts, ranks_ref, u_ref, sum_ref, skew_ref, tail_ref, *refs):
    coefs = refs[: len(shifts)]
    out_ref, slots, sems = refs[len(shifts) :]
    block = slots.shape[1]
    alive = [alive_coef(shift, ranks_ref, coef[...]) for shift, coef in zip(shifts, coefs)]
    copies = []
    for step in range(out_ref.shape[0] // block):
        rows = slice(step * block, (step + 1) * block)
        gaussian = sum_ref[rows, :]
        for shift, coef in zip(shifts, alive):
            columns = coef.shape[0]
            start = pl.multiple_of(source_of(shift) * columns, columns)
            gaussian += jnp.dot(
                u_ref[rows, pl.ds(start, columns)], coef, preferred_element_type=jnp.float32
            )
        skew, tail = skew_ref[rows, :], tail_ref[rows, :]
        growth, turn, scale = LOG2E * skew, 0.5 * skew, 1.0 / skew
        spread = (0.5 * LOG2E) * tail
        lanes = skew.shape[1]
        for start in range(0, gaussian.shape[1], lanes):
            at = gaussian[:, start : start + lanes]
            grown = (jnp.exp2(growth * at) + 1.0) * jnp.tanh(turn * at) * scale
            slots[step, :, start : start + lanes] = grown * jnp.exp2(spread * (at * at))
        copy = pltpu.make_async_copy(slots.at[step], out_ref.at[rows, :], sems.at[step])
        copy.start()
        copies.append(copy)
    for copy in copies:
        copy.wait()


def finish(shifts, ranks, u_whole, total, skew, tail, coefs):
    rows, columns = u_whole.shape
    per_source, reals = coefs[0].shape
    block = min(rows, 128)
    return pl.pallas_call(
        functools.partial(finish_kernel, shifts),
        out_shape=jax.ShapeDtypeStruct((rows, reals), jnp.float32),
        in_specs=[SMEM] + [VMEM] * (4 + len(coefs)),
        out_specs=pl.BlockSpec(memory_space=pl.ANY),
        scratch_shapes=[
            pltpu.VMEM((rows // block, block, reals), jnp.float32),
            pltpu.SemaphoreType.DMA((rows // block,)),
        ],
        compiler_params=vmem((rows, 4 * reals), u_whole.shape),
        cost_estimate=cost(2 * rows * len(coefs) * per_source * reals, u_whole, total, *coefs),
        name="finish",
    )(ranks, u_whole, total, skew, tail, *coefs)


def after(value, *before):
    return lax.optimization_barrier((value, before))[0]


def swap(array, distance):
    count = lax.axis_size("real")
    return lax.ppermute(array, "real", [(k, k ^ distance) for k in range(count)])


def with_other_core(pieces):
    both = dict(pieces)
    for (distance, row), piece in pieces.items():
        if (distance ^ 1, row) not in pieces:
            both[distance ^ 1, row] = swap(piece, 1)
    return both


def from_chips(own):
    pieces = {(0, 0): own}
    for distance in range(2, lax.axis_size("real"), 2):
        pieces[distance, 0] = swap(own, distance)
    return pieces


def from_other_core(pieces):
    return {place: array for place, array in with_other_core(pieces).items() if place not in pieces}


def at_once(gather, pieces):
    places, arrays, new = list(pieces), list(pieces.values()), []

    def added(*arrays):
        more = gather(dict(zip(places, arrays)))
        new[:] = [place for place in more if place not in pieces]
        return [more[place] for place in new]

    count = len(jax.eval_shape(added, *arrays))
    results = lax.cond(lax.axis_index("real") >= 0, added, lambda *same: [same[0]] * count, *arrays)
    return dict(zip(new, results))


def along_site(coef, shift):
    count = lax.axis_size("site")
    return lax.ppermute(coef, "site", [(k, (k + shift) % count) for k in range(count)])


def per_device(noise, v_factors, u_factors, ranks, skew_g, tail_h):
    site_count = lax.axis_size("site")
    real_count = lax.axis_size("real")
    source = lax.axis_index("site")
    rows, columns = v_factors.shape[1:]
    per_dest = columns // site_count
    middle = site_count // 2
    others = sorted(range(1, site_count), key=lambda shift: (abs(shift - middle), shift))
    first, rest = others[0], tuple(others[1:])

    def columns_for(shift):
        start = lax.rem(source + shift, site_count) * per_dest
        return lax.dynamic_slice(v_factors[0], (0, start), (rows, per_dest))

    v_first = columns_for(first)
    v_rest = jnp.concatenate([columns_for(shift) for shift in rest], axis=1)
    own_and_u = jnp.concatenate([columns_for(0), u_factors[0]], axis=1)
    v_first = from_chips(v_first)
    last = max(v_first)
    waiting = (v_first[last], stage(noise), v_rest, own_and_u)
    v_first[last], noise_here, v_rest, own_and_u = lax.optimization_barrier(waiting)
    [far] = project(1, noise_here, with_other_core(v_first).items())

    u_swapped = swap(after(own_and_u, far), 1)
    v_pieces = {(0, 0): after(v_rest, far, u_swapped)}
    v_pieces.update(at_once(lambda own: with_other_core(from_chips(own[0, 0])), v_pieces))
    u_pieces = {**from_chips(after(own_and_u, v_pieces)), (1, 0): u_swapped}
    others = project(len(rest), noise_here, v_pieces.items())
    far = along_site(far, first)
    others = [others[0], *after(others[1:], far)]
    u_pieces.update(at_once(from_other_core, u_pieces))
    others = [along_site(coef, shift) for coef, shift in zip(others, rest)]
    u_whole, total, skew, tail = accumulate(
        (first,), ranks, noise, skew_g[None], tail_h[None], u_pieces.items(), [far]
    )
    return finish(rest, ranks, u_whole, total, skew, tail, others)


def solution(mesh):
    placed = (
        P("site", "real"),
        P("site", "real", None),
        P("site", "real", None),
        P(),
        P("site"),
        P("site"),
    )
    return jax.shard_map(
        per_device, mesh=mesh, in_specs=placed, out_specs=P("site", "real"), check_vma=False
    )
```

```python
import functools
import math

import jax
import jax.numpy as jnp
from jax import lax
from jax.experimental import pallas as pl
from jax.experimental.pallas import tpu as pltpu
from jax.sharding import PartitionSpec as P

CAP = 2
LOG2E = 1.4426950408889634
VMEM = pl.BlockSpec(memory_space=pltpu.VMEM)
SMEM = pl.BlockSpec(memory_space=pltpu.SMEM)


def vmem(*shapes):
    held = sum(4 * math.prod(shape) for shape in shapes)
    return pltpu.CompilerParams(vmem_limit_bytes=held + 6 * 2**20)


def cost(flops, *arrays):
    touched = sum(array.size * array.dtype.itemsize for array in arrays)
    return pl.CostEstimate(flops=flops, bytes_accessed=2 * touched, transcendentals=0)


def stack_pieces(places, rows, pieces, whole):
    me = lax.axis_index("real")
    for (distance, row), piece in zip(places, pieces):
        height = piece.shape[0]
        start = pl.multiple_of((me ^ distance) * rows + row, height)
        whole[pl.ds(start, height), :] = piece[...]


def project_columns(v_columns, noise_ref):
    projected = lax.dot_general(
        v_columns, noise_ref[...], (((0,), (0,)), ((), ())), preferred_element_type=jnp.float32
    )
    return projected.astype(jnp.bfloat16)


def project_kernel(places, rows, noise_ref, *refs):
    pieces, outs, whole = refs[: len(places)], refs[len(places) : -1], refs[-1]
    stack_pieces(places, rows, pieces, whole)
    for place, out_ref in enumerate(outs):
        columns = out_ref.shape[0]
        out_ref[...] = project_columns(
            whole[:, place * columns : (place + 1) * columns], noise_ref
        )


def project(n_shifts, noise, gathered):
    sites, reals = noise.shape
    places, pieces = zip(*gathered)
    rows, columns = pieces[0].shape
    return pl.pallas_call(
        functools.partial(project_kernel, places, rows),
        out_shape=[jax.ShapeDtypeStruct((columns // n_shifts, reals), jnp.bfloat16)] * n_shifts,
        in_specs=[VMEM] * (1 + len(pieces)),
        out_specs=[VMEM] * n_shifts,
        scratch_shapes=[pltpu.VMEM((sites, columns), jnp.bfloat16)],
        compiler_params=vmem(noise.shape, (sites, 2 * columns)),
        cost_estimate=cost(2 * sites * columns * reals, noise, *pieces),
        name=f"project_{n_shifts}",
    )(noise, *pieces)


def stage_kernel(from_ref, to_ref, sems):
    parts = sems.shape[0]
    rows = from_ref.shape[0] // parts
    copies = []
    for part in range(parts):
        span = slice(part * rows, (part + 1) * rows)
        copies.append(
            pltpu.make_async_copy(from_ref.at[span, :], to_ref.at[span, :], sems.at[part])
        )
        copies[-1].start()
    for copy in copies:
        copy.wait()


def stage(array):
    return pl.pallas_call(
        stage_kernel,
        out_shape=jax.ShapeDtypeStruct(array.shape, array.dtype),
        in_specs=[pl.BlockSpec(memory_space=pltpu.HBM)],
        out_specs=VMEM,
        scratch_shapes=[pltpu.SemaphoreType.DMA((4,))],
        compiler_params=vmem(array.shape),
        cost_estimate=cost(0, array),
        name="stage",
    )(array)


def source_of(shift):
    site_count = lax.axis_size("site")
    return lax.rem(lax.axis_index("site") + (site_count - shift), site_count)


def alive_coef(shift, ranks_ref, coef):
    rank = ranks_ref[lax.axis_index("site"), source_of(shift)]
    row = lax.broadcasted_iota(jnp.int32, coef.shape, 0)
    alive = row < rank * (coef.shape[0] // CAP)
    return jnp.where(alive, coef.astype(jnp.float32), 0.0).astype(coef.dtype)


def as_rows(ref, rows):
    values = ref[:, rows]
    return jnp.transpose(jnp.broadcast_to(values, (values.shape[1], values.shape[1])))


def accumulate_kernel(shifts, places, rows, ranks_ref, noise_ref, skew_ref, tail_ref, *refs):
    pieces, coefs = refs[: len(places)], refs[len(places) : len(places) + len(shifts)]
    u_ref, sum_ref, skew_rows, tail_rows, whole = refs[-5:]
    stack_pieces(places, rows, pieces, whole)
    per_source = whole.shape[1] - u_ref.shape[1]
    u_ref[...] = whole[:, per_source:]
    own = project_columns(whole[:, :per_source], noise_ref)
    total = jnp.zeros(sum_ref.shape, jnp.float32)
    for shift, coef in zip((0,) + shifts, [own] + [coef_ref[...] for coef_ref in coefs]):
        start = pl.multiple_of(source_of(shift) * per_source, per_source)
        total += jnp.dot(
            u_ref[:, pl.ds(start, per_source)],
            alive_coef(shift, ranks_ref, coef),
            preferred_element_type=jnp.float32,
        )
    sum_ref[...] = total
    lanes = skew_rows.shape[1]
    for start in range(0, skew_rows.shape[0], lanes):
        part = slice(start, start + lanes)
        skew_rows[part, :], tail_rows[part, :] = as_rows(skew_ref, part), as_rows(tail_ref, part)


def accumulate(shifts, ranks, noise, skew, tail, gathered, coefs):
    places, pieces = zip(*gathered)
    sites, reals = noise.shape
    rows, columns = sites // lax.axis_size("real"), pieces[0].shape[1]
    per_source = coefs[0].shape[0]
    return pl.pallas_call(
        functools.partial(accumulate_kernel, shifts, places, rows),
        out_shape=[
            jax.ShapeDtypeStruct((sites, columns - per_source), jnp.bfloat16),
            jax.ShapeDtypeStruct((sites, reals), jnp.float32),
            jax.ShapeDtypeStruct((sites, min(sites, 128)), jnp.float32),
            jax.ShapeDtypeStruct((sites, min(sites, 128)), jnp.float32),
        ],
        in_specs=[SMEM] + [VMEM] * (3 + len(pieces) + len(coefs)),
        out_specs=[VMEM] * 4,
        scratch_shapes=[pltpu.VMEM((sites, columns), jnp.bfloat16)],
        compiler_params=vmem((sites, 3 * reals), (sites, 2 * columns)),
        cost_estimate=cost(6 * sites * per_source * reals, noise, *pieces, *coefs),
        name="accumulate",
    )(ranks, noise, skew, tail, *pieces, *coefs)


def finish_kernel(shifts, ranks_ref, u_ref, sum_ref, skew_ref, tail_ref, *refs):
    coefs = refs[: len(shifts)]
    out_ref, slots, sems = refs[len(shifts) :]
    block = slots.shape[1]
    alive = [alive_coef(shift, ranks_ref, coef[...]) for shift, coef in zip(shifts, coefs)]
    copies = []
    for step in range(out_ref.shape[0] // block):
        rows = slice(step * block, (step + 1) * block)
        gaussian = sum_ref[rows, :]
        for shift, coef in zip(shifts, alive):
            columns = coef.shape[0]
            start = pl.multiple_of(source_of(shift) * columns, columns)
            gaussian += jnp.dot(
                u_ref[rows, pl.ds(start, columns)], coef, preferred_element_type=jnp.float32
            )
        skew, tail = skew_ref[rows, :], tail_ref[rows, :]
        growth, turn, scale = LOG2E * skew, 0.5 * skew, 1.0 / skew
        spread = (0.5 * LOG2E) * tail
        lanes = skew.shape[1]
        for start in range(0, gaussian.shape[1], lanes):
            at = gaussian[:, start : start + lanes]
            grown = (jnp.exp2(growth * at) + 1.0) * jnp.tanh(turn * at) * scale
            slots[step, :, start : start + lanes] = grown * jnp.exp2(spread * (at * at))
        copy = pltpu.make_async_copy(slots.at[step], out_ref.at[rows, :], sems.at[step])
        copy.start()
        copies.append(copy)
    for copy in copies:
        copy.wait()


def finish(shifts, ranks, u_whole, total, skew, tail, coefs):
    rows, columns = u_whole.shape
    per_source, reals = coefs[0].shape
    block = min(rows, 128)
    return pl.pallas_call(
        functools.partial(finish_kernel, shifts),
        out_shape=jax.ShapeDtypeStruct((rows, reals), jnp.float32),
        in_specs=[SMEM] + [VMEM] * (4 + len(coefs)),
        out_specs=pl.BlockSpec(memory_space=pl.ANY),
        scratch_shapes=[
            pltpu.VMEM((rows // block, block, reals), jnp.float32),
            pltpu.SemaphoreType.DMA((rows // block,)),
        ],
        compiler_params=vmem((rows, 4 * reals), u_whole.shape),
        cost_estimate=cost(2 * rows * len(coefs) * per_source * reals, u_whole, total, *coefs),
        name="finish",
    )(ranks, u_whole, total, skew, tail, *coefs)


def after(value, *before):
    return lax.optimization_barrier((value, before))[0]


def swap(array, distance):
    count = lax.axis_size("real")
    return lax.ppermute(array, "real", [(k, k ^ distance) for k in range(count)])


def with_other_core(pieces):
    both = dict(pieces)
    for (distance, row), piece in pieces.items():
        if (distance ^ 1, row) not in pieces:
            both[distance ^ 1, row] = swap(piece, 1)
    return both


def from_chips(own):
    pieces = {(0, 0): own}
    for distance in range(2, lax.axis_size("real"), 2):
        pieces[distance, 0] = swap(own, distance)
    return pieces


def from_other_core(pieces):
    return {place: array for place, array in with_other_core(pieces).items() if place not in pieces}


def at_once(gather, pieces):
    places, arrays, new = list(pieces), list(pieces.values()), []

    def added(*arrays):
        more = gather(dict(zip(places, arrays)))
        new[:] = [place for place in more if place not in pieces]
        return [more[place] for place in new]

    count = len(jax.eval_shape(added, *arrays))
    results = lax.cond(lax.axis_index("real") >= 0, added, lambda *same: [same[0]] * count, *arrays)
    return dict(zip(new, results))


def along_site(coef, shift):
    count = lax.axis_size("site")
    return lax.ppermute(coef, "site", [(k, (k + shift) % count) for k in range(count)])


def per_device(noise, v_factors, u_factors, ranks, skew_g, tail_h):
    site_count = lax.axis_size("site")
    real_count = lax.axis_size("real")
    source = lax.axis_index("site")
    rows, columns = v_factors.shape[1:]
    per_dest = columns // site_count
    middle = site_count // 2
    others = sorted(range(1, site_count), key=lambda shift: (abs(shift - middle), shift))
    first, rest = others[0], tuple(others[1:])

    def columns_for(shift):
        start = lax.rem(source + shift, site_count) * per_dest
        return lax.dynamic_slice(v_factors[0], (0, start), (rows, per_dest))

    v_first = columns_for(first)
    v_rest = jnp.concatenate([columns_for(shift) for shift in rest], axis=1)
    own_and_u = jnp.concatenate([columns_for(0), u_factors[0]], axis=1)
    v_first = from_chips(v_first)
    last = (2, 0)
    waiting = (v_first[last], stage(noise), v_rest, own_and_u)
    v_first[last], noise_here, v_rest, own_and_u = lax.optimization_barrier(waiting)
    [far] = project(1, noise_here, with_other_core(v_first).items())

    u_swapped = swap(after(own_and_u, far), 1)
    v_pieces = {(0, 0): after(v_rest, far, u_swapped)}
    v_pieces.update(at_once(lambda own: with_other_core(from_chips(own[0, 0])), v_pieces))
    u_pieces = {**from_chips(after(own_and_u, v_pieces)), (1, 0): u_swapped}
    others = project(len(rest), noise_here, v_pieces.items())
    far = along_site(far, first)
    others = [others[0], *after(others[1:], far)]
    u_pieces.update(at_once(from_other_core, u_pieces))
    others = [along_site(coef, shift) for coef, shift in zip(others, rest)]
    u_whole, total, skew, tail = accumulate(
        (first,), ranks, noise, skew_g[None], tail_h[None], u_pieces.items(), [far]
    )
    return finish(rest, ranks, u_whole, total, skew, tail, others)


def solution(mesh):
    placed = (
        P("site", "real"),
        P("site", "real", None),
        P("site", "real", None),
        P(),
        P("site"),
        P("site"),
    )
    return jax.shard_map(
        per_device, mesh=mesh, in_specs=placed, out_specs=P("site", "real"), check_vma=False
    )
```

```python
import functools
import math

import jax
import jax.numpy as jnp
from jax import lax
from jax.experimental import pallas as pl
from jax.experimental.pallas import tpu as pltpu
from jax.sharding import PartitionSpec as P

CAP = 2
LOG2E = 1.4426950408889634
VMEM = pl.BlockSpec(memory_space=pltpu.VMEM)
SMEM = pl.BlockSpec(memory_space=pltpu.SMEM)


def vmem(*shapes):
    held = sum(4 * math.prod(shape) for shape in shapes)
    return pltpu.CompilerParams(vmem_limit_bytes=held + 6 * 2**20)


def cost(flops, *arrays):
    touched = sum(array.size * array.dtype.itemsize for array in arrays)
    return pl.CostEstimate(flops=flops, bytes_accessed=2 * touched, transcendentals=0)


def stack_pieces(places, rows, pieces, whole):
    me = lax.axis_index("real")
    for (distance, row), piece in zip(places, pieces):
        height = piece.shape[0]
        start = pl.multiple_of((me ^ distance) * rows + row, height)
        whole[pl.ds(start, height), :] = piece[...]


def project_columns(v_columns, noise_ref):
    projected = lax.dot_general(
        v_columns, noise_ref[...], (((0,), (0,)), ((), ())), preferred_element_type=jnp.float32
    )
    return projected.astype(jnp.bfloat16)


def project_kernel(places, rows, noise_ref, *refs):
    pieces, out_ref, whole = refs[: len(places)], refs[-2], refs[-1]
    stack_pieces(places, rows, pieces, whole)
    out_ref[...] = project_columns(whole[...], noise_ref)


def project(part, parts, noise, gathered):
    sites, reals = noise.shape
    places, pieces = zip(*gathered)
    rows, columns = pieces[0].shape
    columns //= parts
    piece = VMEM if parts == 1 else pl.BlockSpec((rows, columns), lambda _: (0, part))
    return pl.pallas_call(
        functools.partial(project_kernel, places, rows),
        out_shape=jax.ShapeDtypeStruct((columns, reals), jnp.bfloat16),
        grid=(1,),
        in_specs=[VMEM] + [piece] * len(pieces),
        out_specs=VMEM,
        scratch_shapes=[pltpu.VMEM((sites, columns), jnp.bfloat16)],
        compiler_params=vmem(noise.shape, (sites, 2 * columns)),
        cost_estimate=cost(2 * sites * columns * reals, noise, *pieces),
        name=f"project_{parts}",
    )(noise, *pieces)


def stage_kernel(from_ref, to_ref, sems):
    parts = sems.shape[0]
    rows = from_ref.shape[0] // parts
    copies = []
    for part in range(parts):
        span = slice(part * rows, (part + 1) * rows)
        copies.append(
            pltpu.make_async_copy(from_ref.at[span, :], to_ref.at[span, :], sems.at[part])
        )
        copies[-1].start()
    for copy in copies:
        copy.wait()


def stage(array):
    return pl.pallas_call(
        stage_kernel,
        out_shape=jax.ShapeDtypeStruct(array.shape, array.dtype),
        in_specs=[pl.BlockSpec(memory_space=pltpu.HBM)],
        out_specs=VMEM,
        scratch_shapes=[pltpu.SemaphoreType.DMA((4,))],
        compiler_params=vmem(array.shape),
        cost_estimate=cost(0, array),
        name="stage",
    )(array)


def source_of(shift):
    site_count = lax.axis_size("site")
    return lax.rem(lax.axis_index("site") + (site_count - shift), site_count)


def alive_coef(shift, ranks_ref, coef):
    rank = ranks_ref[lax.axis_index("site"), source_of(shift)]
    row = lax.broadcasted_iota(jnp.int32, coef.shape, 0)
    alive = row < rank * (coef.shape[0] // CAP)
    return jnp.where(alive, coef.astype(jnp.float32), 0.0).astype(coef.dtype)


def as_rows(ref, rows):
    values = ref[:, rows]
    return jnp.transpose(jnp.broadcast_to(values, (values.shape[1], values.shape[1])))


def accumulate_kernel(shifts, places, rows, ranks_ref, noise_ref, skew_ref, tail_ref, *refs):
    pieces, coefs = refs[: len(places)], refs[len(places) : len(places) + len(shifts)]
    u_ref, sum_ref, skew_rows, tail_rows, whole = refs[-5:]
    stack_pieces(places, rows, pieces, whole)
    per_source = whole.shape[1] - u_ref.shape[1]
    u_ref[...] = whole[:, per_source:]
    own = project_columns(whole[:, :per_source], noise_ref)
    total = jnp.zeros(sum_ref.shape, jnp.float32)
    for shift, coef in zip((0,) + shifts, [own] + [coef_ref[...] for coef_ref in coefs]):
        start = pl.multiple_of(source_of(shift) * per_source, per_source)
        total += jnp.dot(
            u_ref[:, pl.ds(start, per_source)],
            alive_coef(shift, ranks_ref, coef),
            preferred_element_type=jnp.float32,
        )
    sum_ref[...] = total
    lanes = skew_rows.shape[1]
    for start in range(0, skew_rows.shape[0], lanes):
        part = slice(start, start + lanes)
        skew_rows[part, :], tail_rows[part, :] = as_rows(skew_ref, part), as_rows(tail_ref, part)


def accumulate(shifts, ranks, noise, skew, tail, gathered, coefs):
    places, pieces = zip(*gathered)
    sites, reals = noise.shape
    rows, columns = sites // lax.axis_size("real"), pieces[0].shape[1]
    per_source = coefs[0].shape[0]
    return pl.pallas_call(
        functools.partial(accumulate_kernel, shifts, places, rows),
        out_shape=[
            jax.ShapeDtypeStruct((sites, columns - per_source), jnp.bfloat16),
            jax.ShapeDtypeStruct((sites, reals), jnp.float32),
            jax.ShapeDtypeStruct((sites, min(sites, 128)), jnp.float32),
            jax.ShapeDtypeStruct((sites, min(sites, 128)), jnp.float32),
        ],
        in_specs=[SMEM] + [VMEM] * (3 + len(pieces) + len(coefs)),
        out_specs=[VMEM] * 4,
        scratch_shapes=[pltpu.VMEM((sites, columns), jnp.bfloat16)],
        compiler_params=vmem((sites, 3 * reals), (sites, 2 * columns)),
        cost_estimate=cost(6 * sites * per_source * reals, noise, *pieces, *coefs),
        name="accumulate",
    )(ranks, noise, skew, tail, *pieces, *coefs)


def finish_kernel(shifts, ranks_ref, u_ref, sum_ref, skew_ref, tail_ref, *refs):
    coefs = refs[: len(shifts)]
    out_ref, slots, sems = refs[len(shifts) :]
    block = slots.shape[1]
    alive = [alive_coef(shift, ranks_ref, coef[...]) for shift, coef in zip(shifts, coefs)]
    copies = []
    for step in range(out_ref.shape[0] // block):
        rows = slice(step * block, (step + 1) * block)
        gaussian = sum_ref[rows, :]
        for shift, coef in zip(shifts, alive):
            columns = coef.shape[0]
            start = pl.multiple_of(source_of(shift) * columns, columns)
            gaussian += jnp.dot(
                u_ref[rows, pl.ds(start, columns)], coef, preferred_element_type=jnp.float32
            )
        skew, tail = skew_ref[rows, :], tail_ref[rows, :]
        growth, turn, scale = LOG2E * skew, 0.5 * skew, 1.0 / skew
        spread = (0.5 * LOG2E) * tail
        lanes = skew.shape[1]
        for start in range(0, gaussian.shape[1], lanes):
            at = gaussian[:, start : start + lanes]
            grown = (jnp.exp2(growth * at) + 1.0) * jnp.tanh(turn * at) * scale
            slots[step, :, start : start + lanes] = grown * jnp.exp2(spread * (at * at))
        copy = pltpu.make_async_copy(slots.at[step], out_ref.at[rows, :], sems.at[step])
        copy.start()
        copies.append(copy)
    for copy in copies:
        copy.wait()


def finish(shifts, ranks, u_whole, total, skew, tail, coefs):
    rows, columns = u_whole.shape
    per_source, reals = coefs[0].shape
    block = min(rows, 128)
    return pl.pallas_call(
        functools.partial(finish_kernel, shifts),
        out_shape=jax.ShapeDtypeStruct((rows, reals), jnp.float32),
        in_specs=[SMEM] + [VMEM] * (4 + len(coefs)),
        out_specs=pl.BlockSpec(memory_space=pl.ANY),
        scratch_shapes=[
            pltpu.VMEM((rows // block, block, reals), jnp.float32),
            pltpu.SemaphoreType.DMA((rows // block,)),
        ],
        compiler_params=vmem((rows, 4 * reals), u_whole.shape),
        cost_estimate=cost(2 * rows * len(coefs) * per_source * reals, u_whole, total, *coefs),
        name="finish",
    )(ranks, u_whole, total, skew, tail, *coefs)


def after(value, *before):
    return lax.optimization_barrier((value, before))[0]


def swap(array, distance):
    count = lax.axis_size("real")
    return lax.ppermute(array, "real", [(k, k ^ distance) for k in range(count)])


def with_other_core(pieces):
    both = dict(pieces)
    for (distance, row), piece in pieces.items():
        if (distance ^ 1, row) not in pieces:
            both[distance ^ 1, row] = swap(piece, 1)
    return both


def from_chips(own):
    pieces = {(0, 0): own}
    for distance in range(2, lax.axis_size("real"), 2):
        pieces[distance, 0] = swap(own, distance)
    return pieces


def from_other_core(pieces):
    return {place: array for place, array in with_other_core(pieces).items() if place not in pieces}


def at_once(gather, pieces):
    places, arrays, new = list(pieces), list(pieces.values()), []

    def added(*arrays):
        more = gather(dict(zip(places, arrays)))
        new[:] = [place for place in more if place not in pieces]
        return [more[place] for place in new]

    count = len(jax.eval_shape(added, *arrays))
    results = lax.cond(lax.axis_index("real") >= 0, added, lambda *same: [same[0]] * count, *arrays)
    return dict(zip(new, results))


def along_site(coef, shift):
    count = lax.axis_size("site")
    return lax.ppermute(coef, "site", [(k, (k + shift) % count) for k in range(count)])


def per_device(noise, v_factors, u_factors, ranks, skew_g, tail_h):
    site_count = lax.axis_size("site")
    real_count = lax.axis_size("real")
    source = lax.axis_index("site")
    rows, columns = v_factors.shape[1:]
    per_dest = columns // site_count
    middle = site_count // 2
    others = sorted(range(1, site_count), key=lambda shift: (abs(shift - middle), shift))
    first, rest = others[0], tuple(others[1:])

    def columns_for(shift):
        start = lax.rem(source + shift, site_count) * per_dest
        return lax.dynamic_slice(v_factors[0], (0, start), (rows, per_dest))

    v_first = columns_for(first)
    v_rest = jnp.concatenate([columns_for(shift) for shift in rest], axis=1)
    own_and_u = jnp.concatenate([columns_for(0), u_factors[0]], axis=1)
    v_first = from_chips(v_first)
    last = (2, 0)
    waiting = (v_first[last], stage(noise), v_rest, own_and_u)
    v_first[last], noise_here, v_rest, own_and_u = lax.optimization_barrier(waiting)
    far = project(0, 1, noise_here, with_other_core(v_first).items())

    u_swapped = swap(after(own_and_u, far), 1)
    v_pieces = {(0, 0): after(v_rest, far, u_swapped)}
    v_pieces.update(at_once(lambda own: with_other_core(from_chips(own[0, 0])), v_pieces))
    u_pieces = {**from_chips(after(own_and_u, v_pieces)), (1, 0): u_swapped}
    others = [project(0, len(rest), noise_here, v_pieces.items())]
    far = along_site(far, first)
    noise_here = after(noise_here, far, others[0])
    for part in range(1, len(rest)):
        others.append(project(part, len(rest), noise_here, v_pieces.items()))
    u_pieces = after(u_pieces, others[-1])
    u_pieces.update(at_once(from_other_core, u_pieces))
    others = [along_site(coef, shift) for coef, shift in zip(others, rest)]
    u_whole, total, skew, tail = accumulate(
        (first,), ranks, noise, skew_g[None], tail_h[None], u_pieces.items(), [far]
    )
    return finish(rest, ranks, u_whole, total, skew, tail, others)


def solution(mesh):
    placed = (
        P("site", "real"),
        P("site", "real", None),
        P("site", "real", None),
        P(),
        P("site"),
        P("site"),
    )
    return jax.shard_map(
        per_device, mesh=mesh, in_specs=placed, out_specs=P("site", "real"), check_vma=False
    )
```

```python
import functools
import math

import jax
import jax.numpy as jnp
from jax import lax
from jax.experimental import pallas as pl
from jax.experimental.pallas import tpu as pltpu
from jax.sharding import PartitionSpec as P

CAP = 2
LOG2E = 1.4426950408889634
VMEM = pl.BlockSpec(memory_space=pltpu.VMEM)
SMEM = pl.BlockSpec(memory_space=pltpu.SMEM)


def vmem(*shapes):
    held = sum(4 * math.prod(shape) for shape in shapes)
    return pltpu.CompilerParams(vmem_limit_bytes=held + 6 * 2**20)


def cost(flops, *arrays):
    touched = sum(array.size * array.dtype.itemsize for array in arrays)
    return pl.CostEstimate(flops=flops, bytes_accessed=2 * touched, transcendentals=0)


def stack_pieces(places, rows, pieces, whole):
    me = lax.axis_index("real")
    for (distance, row), piece in zip(places, pieces):
        height = piece.shape[0]
        start = pl.multiple_of((me ^ distance) * rows + row, height)
        whole[pl.ds(start, height), :] = piece[...]


def project_columns(v_columns, noise_ref):
    projected = lax.dot_general(
        v_columns, noise_ref[...], (((0,), (0,)), ((), ())), preferred_element_type=jnp.float32
    )
    return projected.astype(jnp.bfloat16)


def project_kernel(places, rows, noise_ref, *refs):
    pieces, outs, whole = refs[: len(places)], refs[len(places) : -1], refs[-1]
    stack_pieces(places, rows, pieces, whole)
    for place, out_ref in enumerate(outs):
        columns = out_ref.shape[0]
        out_ref[...] = project_columns(
            whole[:, place * columns : (place + 1) * columns], noise_ref
        )


def project(n_shifts, noise, gathered):
    sites, reals = noise.shape
    places, pieces = zip(*gathered)
    rows, columns = pieces[0].shape
    return pl.pallas_call(
        functools.partial(project_kernel, places, rows),
        out_shape=[jax.ShapeDtypeStruct((columns // n_shifts, reals), jnp.bfloat16)] * n_shifts,
        in_specs=[VMEM] * (1 + len(pieces)),
        out_specs=[VMEM] * n_shifts,
        scratch_shapes=[pltpu.VMEM((sites, columns), jnp.bfloat16)],
        compiler_params=vmem(noise.shape, (sites, 2 * columns)),
        cost_estimate=cost(2 * sites * columns * reals, noise, *pieces),
        name=f"project_{n_shifts}",
    )(noise, *pieces)


def stage_kernel(from_ref, to_ref, sems):
    parts = sems.shape[0]
    rows = from_ref.shape[0] // parts
    copies = []
    for part in range(parts):
        span = slice(part * rows, (part + 1) * rows)
        copies.append(
            pltpu.make_async_copy(from_ref.at[span, :], to_ref.at[span, :], sems.at[part])
        )
        copies[-1].start()
    for copy in copies:
        copy.wait()


def stage(array):
    return pl.pallas_call(
        stage_kernel,
        out_shape=jax.ShapeDtypeStruct(array.shape, array.dtype),
        in_specs=[pl.BlockSpec(memory_space=pltpu.HBM)],
        out_specs=VMEM,
        scratch_shapes=[pltpu.SemaphoreType.DMA((4,))],
        compiler_params=vmem(array.shape),
        cost_estimate=cost(0, array),
        name="stage",
    )(array)


def source_of(shift):
    site_count = lax.axis_size("site")
    return lax.rem(lax.axis_index("site") + (site_count - shift), site_count)


def alive_coef(shift, ranks_ref, coef):
    rank = ranks_ref[lax.axis_index("site"), source_of(shift)]
    row = lax.broadcasted_iota(jnp.int32, coef.shape, 0)
    alive = row < rank * (coef.shape[0] // CAP)
    return jnp.where(alive, coef.astype(jnp.float32), 0.0).astype(coef.dtype)


def as_rows(ref, rows):
    values = ref[:, rows]
    return jnp.transpose(jnp.broadcast_to(values, (values.shape[1], values.shape[1])))


def accumulate_kernel(shifts, places, rows, ranks_ref, noise_ref, skew_ref, tail_ref, *refs):
    pieces, coefs = refs[: len(places)], refs[len(places) : len(places) + len(shifts)]
    u_ref, sum_ref, skew_rows, tail_rows, whole = refs[-5:]
    stack_pieces(places, rows, pieces, whole)
    per_source = whole.shape[1] - u_ref.shape[1]
    u_ref[...] = whole[:, per_source:]
    own = project_columns(whole[:, :per_source], noise_ref)
    total = jnp.zeros(sum_ref.shape, jnp.float32)
    for shift, coef in zip((0,) + shifts, [own] + [coef_ref[...] for coef_ref in coefs]):
        start = pl.multiple_of(source_of(shift) * per_source, per_source)
        total += jnp.dot(
            u_ref[:, pl.ds(start, per_source)],
            alive_coef(shift, ranks_ref, coef),
            preferred_element_type=jnp.float32,
        )
    sum_ref[...] = total
    lanes = skew_rows.shape[1]
    for start in range(0, skew_rows.shape[0], lanes):
        part = slice(start, start + lanes)
        skew_rows[part, :], tail_rows[part, :] = as_rows(skew_ref, part), as_rows(tail_ref, part)


def accumulate(shifts, ranks, noise, skew, tail, gathered, coefs):
    places, pieces = zip(*gathered)
    sites, reals = noise.shape
    rows, columns = sites // lax.axis_size("real"), pieces[0].shape[1]
    per_source = coefs[0].shape[0]
    return pl.pallas_call(
        functools.partial(accumulate_kernel, shifts, places, rows),
        out_shape=[
            jax.ShapeDtypeStruct((sites, columns - per_source), jnp.bfloat16),
            jax.ShapeDtypeStruct((sites, reals), jnp.float32),
            jax.ShapeDtypeStruct((sites, min(sites, 128)), jnp.float32),
            jax.ShapeDtypeStruct((sites, min(sites, 128)), jnp.float32),
        ],
        in_specs=[SMEM] + [VMEM] * (3 + len(pieces) + len(coefs)),
        out_specs=[VMEM] * 4,
        scratch_shapes=[pltpu.VMEM((sites, columns), jnp.bfloat16)],
        compiler_params=vmem((sites, 3 * reals), (sites, 2 * columns)),
        cost_estimate=cost(6 * sites * per_source * reals, noise, *pieces, *coefs),
        name="accumulate",
    )(ranks, noise, skew, tail, *pieces, *coefs)


def finish_kernel(shifts, ranks_ref, u_ref, sum_ref, skew_ref, tail_ref, *refs):
    coefs = refs[: len(shifts)]
    out_ref, slots, sems = refs[len(shifts) :]
    block = slots.shape[1]
    alive = [alive_coef(shift, ranks_ref, coef[...]) for shift, coef in zip(shifts, coefs)]
    copies = []
    for step in range(out_ref.shape[0] // block):
        rows = slice(step * block, (step + 1) * block)
        gaussian = sum_ref[rows, :]
        for shift, coef in zip(shifts, alive):
            columns = coef.shape[0]
            start = pl.multiple_of(source_of(shift) * columns, columns)
            gaussian += jnp.dot(
                u_ref[rows, pl.ds(start, columns)], coef, preferred_element_type=jnp.float32
            )
        skew, tail = skew_ref[rows, :], tail_ref[rows, :]
        growth, turn, scale = LOG2E * skew, 0.5 * skew, 1.0 / skew
        spread = (0.5 * LOG2E) * tail
        lanes = skew.shape[1]
        for start in range(0, gaussian.shape[1], lanes):
            at = gaussian[:, start : start + lanes]
            grown = (jnp.exp2(growth * at) + 1.0) * jnp.tanh(turn * at) * scale
            slots[step, :, start : start + lanes] = grown * jnp.exp2(spread * (at * at))
        copy = pltpu.make_async_copy(slots.at[step], out_ref.at[rows, :], sems.at[step])
        copy.start()
        copies.append(copy)
    for copy in copies:
        copy.wait()


def finish(shifts, ranks, u_whole, total, skew, tail, coefs):
    rows, columns = u_whole.shape
    per_source, reals = coefs[0].shape
    block = min(rows, 128)
    return pl.pallas_call(
        functools.partial(finish_kernel, shifts),
        out_shape=jax.ShapeDtypeStruct((rows, reals), jnp.float32),
        in_specs=[SMEM] + [VMEM] * (4 + len(coefs)),
        out_specs=pl.BlockSpec(memory_space=pl.ANY),
        scratch_shapes=[
            pltpu.VMEM((rows // block, block, reals), jnp.float32),
            pltpu.SemaphoreType.DMA((rows // block,)),
        ],
        compiler_params=vmem((rows, 4 * reals), u_whole.shape),
        cost_estimate=cost(2 * rows * len(coefs) * per_source * reals, u_whole, total, *coefs),
        name="finish",
    )(ranks, u_whole, total, skew, tail, *coefs)


def after(value, *before):
    return lax.optimization_barrier((value, before))[0]


def swap(array, distance):
    count = lax.axis_size("real")
    return lax.ppermute(array, "real", [(k, k ^ distance) for k in range(count)])


def with_other_core(pieces):
    both = dict(pieces)
    for (distance, row), piece in pieces.items():
        if (distance ^ 1, row) not in pieces:
            both[distance ^ 1, row] = swap(piece, 1)
    return both


def from_chips(own):
    pieces = {(0, 0): own}
    for distance in range(2, lax.axis_size("real"), 2):
        pieces[distance, 0] = swap(own, distance)
    return pieces


def from_other_core(pieces):
    return {place: array for place, array in with_other_core(pieces).items() if place not in pieces}


def at_once(gather, pieces):
    places, arrays, new = list(pieces), list(pieces.values()), []

    def added(*arrays):
        more = gather(dict(zip(places, arrays)))
        new[:] = [place for place in more if place not in pieces]
        return [more[place] for place in new]

    count = len(jax.eval_shape(added, *arrays))
    results = lax.cond(lax.axis_index("real") >= 0, added, lambda *same: [same[0]] * count, *arrays)
    return dict(zip(new, results))


def along_site(coef, shift):
    count = lax.axis_size("site")
    return lax.ppermute(coef, "site", [(k, (k + shift) % count) for k in range(count)])


def per_device(noise, v_factors, u_factors, ranks, skew_g, tail_h):
    site_count = lax.axis_size("site")
    real_count = lax.axis_size("real")
    source = lax.axis_index("site")
    rows, columns = v_factors.shape[1:]
    per_dest = columns // site_count
    middle = site_count // 2
    others = sorted(range(1, site_count), key=lambda shift: (abs(shift - middle), shift))
    first, rest = others[0], tuple(others[1:])

    def columns_for(shift):
        start = lax.rem(source + shift, site_count) * per_dest
        return lax.dynamic_slice(v_factors[0], (0, start), (rows, per_dest))

    v_first = columns_for(first)
    v_rest = jnp.concatenate([columns_for(shift) for shift in rest], axis=1)
    own_and_u = jnp.concatenate([columns_for(0), u_factors[0]], axis=1)
    v_first = from_chips(v_first)
    last = (2, 0)
    waiting = (v_first[last], stage(noise), v_rest, own_and_u)
    v_first[last], noise_here, v_rest, own_and_u = lax.optimization_barrier(waiting)
    [far] = project(1, noise_here, with_other_core(v_first).items())

    v_pieces = {(0, 0): after(v_rest, far)}
    v_pieces.update(at_once(lambda own: with_other_core(from_chips(own[0, 0])), v_pieces))
    own_and_u = after(own_and_u, v_pieces)
    u_pieces = {**from_chips(own_and_u), (1, 0): swap(own_and_u, 1)}
    others = project(len(rest), noise_here, v_pieces.items())
    others, u_pieces[1, 0] = lax.optimization_barrier((others, u_pieces[1, 0]))
    far = along_site(far, first)
    others = [others[0], *after(others[1:], far)]
    u_pieces.update(at_once(from_other_core, u_pieces))
    others = [along_site(coef, shift) for coef, shift in zip(others, rest)]
    u_whole, total, skew, tail = accumulate(
        (first,), ranks, noise, skew_g[None], tail_h[None], u_pieces.items(), [far]
    )
    return finish(rest, ranks, u_whole, total, skew, tail, others)


def solution(mesh):
    placed = (
        P("site", "real"),
        P("site", "real", None),
        P("site", "real", None),
        P(),
        P("site"),
        P("site"),
    )
    return jax.shard_map(
        per_device, mesh=mesh, in_specs=placed, out_specs=P("site", "real"), check_vma=False
    )
```

```python
import functools
import math

import jax
import jax.numpy as jnp
from jax import lax
from jax.experimental import pallas as pl
from jax.experimental.pallas import tpu as pltpu
from jax.sharding import PartitionSpec as P

CAP = 2
LOG2E = 1.4426950408889634
VMEM = pl.BlockSpec(memory_space=pltpu.VMEM)
SMEM = pl.BlockSpec(memory_space=pltpu.SMEM)


def vmem(*shapes):
    held = sum(4 * math.prod(shape) for shape in shapes)
    return pltpu.CompilerParams(vmem_limit_bytes=held + 6 * 2**20)


def cost(flops, *arrays):
    touched = sum(array.size * array.dtype.itemsize for array in arrays)
    return pl.CostEstimate(flops=flops, bytes_accessed=2 * touched, transcendentals=0)


def stack_pieces(places, rows, pieces, whole):
    me = lax.axis_index("real")
    for (distance, row), piece in zip(places, pieces):
        height = piece.shape[0]
        start = pl.multiple_of((me ^ distance) * rows + row, height)
        whole[pl.ds(start, height), :] = piece[...]


def project_columns(v_columns, noise_ref):
    projected = lax.dot_general(
        v_columns, noise_ref[...], (((0,), (0,)), ((), ())), preferred_element_type=jnp.float32
    )
    return projected.astype(jnp.bfloat16)


def project_kernel(places, rows, noise_ref, *refs):
    pieces, outs, whole = refs[: len(places)], refs[len(places) : -1], refs[-1]
    stack_pieces(places, rows, pieces, whole)
    for place, out_ref in enumerate(outs):
        columns = out_ref.shape[0]
        out_ref[...] = project_columns(
            whole[:, place * columns : (place + 1) * columns], noise_ref
        )


def project(n_shifts, noise, gathered):
    sites, reals = noise.shape
    places, pieces = zip(*gathered)
    rows, columns = pieces[0].shape
    return pl.pallas_call(
        functools.partial(project_kernel, places, rows),
        out_shape=[jax.ShapeDtypeStruct((columns // n_shifts, reals), jnp.bfloat16)] * n_shifts,
        in_specs=[VMEM] * (1 + len(pieces)),
        out_specs=[VMEM] * n_shifts,
        scratch_shapes=[pltpu.VMEM((sites, columns), jnp.bfloat16)],
        compiler_params=vmem(noise.shape, (sites, 2 * columns)),
        cost_estimate=cost(2 * sites * columns * reals, noise, *pieces),
        name=f"project_{n_shifts}",
    )(noise, *pieces)


def stage_kernel(from_ref, to_ref, sems):
    parts = sems.shape[0]
    rows = from_ref.shape[0] // parts
    copies = []
    for part in range(parts):
        span = slice(part * rows, (part + 1) * rows)
        copies.append(
            pltpu.make_async_copy(from_ref.at[span, :], to_ref.at[span, :], sems.at[part])
        )
        copies[-1].start()
    for copy in copies:
        copy.wait()


def stage(array):
    return pl.pallas_call(
        stage_kernel,
        out_shape=jax.ShapeDtypeStruct(array.shape, array.dtype),
        in_specs=[pl.BlockSpec(memory_space=pltpu.HBM)],
        out_specs=VMEM,
        scratch_shapes=[pltpu.SemaphoreType.DMA((4,))],
        compiler_params=vmem(array.shape),
        cost_estimate=cost(0, array),
        name="stage",
    )(array)


def source_of(shift):
    site_count = lax.axis_size("site")
    return lax.rem(lax.axis_index("site") + (site_count - shift), site_count)


def alive_coef(shift, ranks_ref, coef):
    rank = ranks_ref[lax.axis_index("site"), source_of(shift)]
    row = lax.broadcasted_iota(jnp.int32, coef.shape, 0)
    alive = row < rank * (coef.shape[0] // CAP)
    return jnp.where(alive, coef.astype(jnp.float32), 0.0).astype(coef.dtype)


def as_rows(ref, rows):
    values = ref[:, rows]
    return jnp.transpose(jnp.broadcast_to(values, (values.shape[1], values.shape[1])))


def accumulate_kernel(shifts, places, rows, ranks_ref, noise_ref, skew_ref, tail_ref, *refs):
    pieces, coefs = refs[: len(places)], refs[len(places) : len(places) + len(shifts)]
    u_ref, sum_ref, skew_rows, tail_rows, whole = refs[-5:]
    stack_pieces(places, rows, pieces, whole)
    per_source = whole.shape[1] - u_ref.shape[1]
    u_ref[...] = whole[:, per_source:]
    own = project_columns(whole[:, :per_source], noise_ref)
    total = jnp.zeros(sum_ref.shape, jnp.float32)
    for shift, coef in zip((0,) + shifts, [own] + [coef_ref[...] for coef_ref in coefs]):
        start = pl.multiple_of(source_of(shift) * per_source, per_source)
        total += jnp.dot(
            u_ref[:, pl.ds(start, per_source)],
            alive_coef(shift, ranks_ref, coef),
            preferred_element_type=jnp.float32,
        )
    sum_ref[...] = total
    lanes = skew_rows.shape[1]
    for start in range(0, skew_rows.shape[0], lanes):
        part = slice(start, start + lanes)
        skew_rows[part, :], tail_rows[part, :] = as_rows(skew_ref, part), as_rows(tail_ref, part)


def accumulate(shifts, ranks, noise, skew, tail, gathered, coefs):
    places, pieces = zip(*gathered)
    sites, reals = noise.shape
    rows, columns = sites // lax.axis_size("real"), pieces[0].shape[1]
    per_source = coefs[0].shape[0]
    return pl.pallas_call(
        functools.partial(accumulate_kernel, shifts, places, rows),
        out_shape=[
            jax.ShapeDtypeStruct((sites, columns - per_source), jnp.bfloat16),
            jax.ShapeDtypeStruct((sites, reals), jnp.float32),
            jax.ShapeDtypeStruct((sites, min(sites, 128)), jnp.float32),
            jax.ShapeDtypeStruct((sites, min(sites, 128)), jnp.float32),
        ],
        in_specs=[SMEM] + [VMEM] * (3 + len(pieces) + len(coefs)),
        out_specs=[VMEM] * 4,
        scratch_shapes=[pltpu.VMEM((sites, columns), jnp.bfloat16)],
        compiler_params=vmem((sites, 3 * reals), (sites, 2 * columns)),
        cost_estimate=cost(6 * sites * per_source * reals, noise, *pieces, *coefs),
        name="accumulate",
    )(ranks, noise, skew, tail, *pieces, *coefs)


def finish_kernel(shifts, ranks_ref, u_ref, sum_ref, skew_ref, tail_ref, *refs):
    coefs = refs[: len(shifts)]
    out_ref, slots, sems = refs[len(shifts) :]
    block = slots.shape[1]
    alive = [alive_coef(shift, ranks_ref, coef[...]) for shift, coef in zip(shifts, coefs)]
    copies = []
    for step in range(out_ref.shape[0] // block):
        rows = slice(step * block, (step + 1) * block)
        gaussian = sum_ref[rows, :]
        for shift, coef in zip(shifts, alive):
            columns = coef.shape[0]
            start = pl.multiple_of(source_of(shift) * columns, columns)
            gaussian += jnp.dot(
                u_ref[rows, pl.ds(start, columns)], coef, preferred_element_type=jnp.float32
            )
        skew, tail = skew_ref[rows, :], tail_ref[rows, :]
        growth, turn, scale = LOG2E * skew, 0.5 * skew, 1.0 / skew
        spread = (0.5 * LOG2E) * tail
        lanes = skew.shape[1]
        for start in range(0, gaussian.shape[1], lanes):
            at = gaussian[:, start : start + lanes]
            grown = (jnp.exp2(growth * at) + 1.0) * jnp.tanh(turn * at) * scale
            slots[step, :, start : start + lanes] = grown * jnp.exp2(spread * (at * at))
        copy = pltpu.make_async_copy(slots.at[step], out_ref.at[rows, :], sems.at[step])
        copy.start()
        copies.append(copy)
    for copy in copies:
        copy.wait()


def finish(shifts, ranks, u_whole, total, skew, tail, coefs):
    rows, columns = u_whole.shape
    per_source, reals = coefs[0].shape
    block = min(rows, 256)
    return pl.pallas_call(
        functools.partial(finish_kernel, shifts),
        out_shape=jax.ShapeDtypeStruct((rows, reals), jnp.float32),
        in_specs=[SMEM] + [VMEM] * (4 + len(coefs)),
        out_specs=pl.BlockSpec(memory_space=pl.ANY),
        scratch_shapes=[
            pltpu.VMEM((rows // block, block, reals), jnp.float32),
            pltpu.SemaphoreType.DMA((rows // block,)),
        ],
        compiler_params=vmem((rows, 4 * reals), u_whole.shape),
        cost_estimate=cost(2 * rows * len(coefs) * per_source * reals, u_whole, total, *coefs),
        name="finish",
    )(ranks, u_whole, total, skew, tail, *coefs)


def after(value, *before):
    return lax.optimization_barrier((value, before))[0]


def swap(array, distance):
    count = lax.axis_size("real")
    return lax.ppermute(array, "real", [(k, k ^ distance) for k in range(count)])


def with_other_core(pieces):
    both = dict(pieces)
    for (distance, row), piece in pieces.items():
        if (distance ^ 1, row) not in pieces:
            both[distance ^ 1, row] = swap(piece, 1)
    return both


def from_chips(own):
    pieces = {(0, 0): own}
    for distance in range(2, lax.axis_size("real"), 2):
        pieces[distance, 0] = swap(own, distance)
    return pieces


def from_other_core(pieces):
    return {place: array for place, array in with_other_core(pieces).items() if place not in pieces}


def at_once(gather, pieces):
    places, arrays, new = list(pieces), list(pieces.values()), []

    def added(*arrays):
        more = gather(dict(zip(places, arrays)))
        new[:] = [place for place in more if place not in pieces]
        return [more[place] for place in new]

    count = len(jax.eval_shape(added, *arrays))
    results = lax.cond(lax.axis_index("real") >= 0, added, lambda *same: [same[0]] * count, *arrays)
    return dict(zip(new, results))


def along_site(coef, shift):
    count = lax.axis_size("site")
    return lax.ppermute(coef, "site", [(k, (k + shift) % count) for k in range(count)])


def per_device(noise, v_factors, u_factors, ranks, skew_g, tail_h):
    site_count = lax.axis_size("site")
    real_count = lax.axis_size("real")
    source = lax.axis_index("site")
    rows, columns = v_factors.shape[1:]
    per_dest = columns // site_count
    middle = site_count // 2
    others = sorted(range(1, site_count), key=lambda shift: (abs(shift - middle), shift))
    first, rest = others[0], tuple(others[1:])

    def columns_for(shift):
        start = lax.rem(source + shift, site_count) * per_dest
        return lax.dynamic_slice(v_factors[0], (0, start), (rows, per_dest))

    v_first = columns_for(first)
    v_rest = jnp.concatenate([columns_for(shift) for shift in rest], axis=1)
    own_and_u = jnp.concatenate([columns_for(0), u_factors[0]], axis=1)
    v_first = from_chips(v_first)
    last = (2, 0)
    waiting = (v_first[last], stage(noise), v_rest, own_and_u)
    v_first[last], noise_here, v_rest, own_and_u = lax.optimization_barrier(waiting)
    [far] = project(1, noise_here, with_other_core(v_first).items())

    u_swapped = swap(after(own_and_u, far), 1)
    v_pieces = {(0, 0): after(v_rest, far, u_swapped)}
    v_pieces.update(at_once(lambda own: with_other_core(from_chips(own[0, 0])), v_pieces))
    u_pieces = {**from_chips(after(own_and_u, v_pieces)), (1, 0): u_swapped}
    others = project(len(rest), noise_here, v_pieces.items())
    far = along_site(far, first)
    others = [others[0], *after(others[1:], far)]
    u_pieces.update(at_once(from_other_core, u_pieces))
    others = [along_site(coef, shift) for coef, shift in zip(others, rest)]
    u_whole, total, skew, tail = accumulate(
        (first,), ranks, noise, skew_g[None], tail_h[None], u_pieces.items(), [far]
    )
    return finish(rest, ranks, u_whole, total, skew, tail, others)


def solution(mesh):
    placed = (
        P("site", "real"),
        P("site", "real", None),
        P("site", "real", None),
        P(),
        P("site"),
        P("site"),
    )
    return jax.shard_map(
        per_device, mesh=mesh, in_specs=placed, out_specs=P("site", "real"), check_vma=False
    )
```
